256 devices in a mesh: shot: 2 (over z_hi), tx: 8 (over z_lo, core), ty: 16 (over x, y).
Axes of the slice: x: 4, y: 4, z: 8 (z_hi: 2, z_lo: 4; z = z_hi * 4 + z_lo), core: 2. Of those that a mesh axis runs over, the one named last changes fastest.
Arguments:
- perturbation: float32 [128, 128, 256], P(('tx', 'ty')), may hold values from -6 to 6
- courant_sq: float32 [128, 256, 128], P('tx', 'ty'), may hold values from 0.08 to 0.3
- background_prev: float32 [2, 128, 256, 128], P('shot', 'tx', 'ty'), may hold values from -6 to 6
- background_now: float32 [2, 128, 256, 128], P('shot', 'tx', 'ty'), may hold values from -6 to 6
- born_prev: float32 [2, 128, 256, 128], P('shot', 'tx', 'ty'), may hold values from -6 to 6
- born_now: float32 [2, 128, 256, 128], P('shot', 'tx', 'ty'), may hold values from -6 to 6
- adjoint_next: float32 [2, 128, 256, 128], P('shot', 'tx', 'ty'), may hold values from -6 to 6
- adjoint_after: float32 [2, 128, 256, 128], P('shot', 'tx', 'ty'), may hold values from -6 to 6
- encode_bits: int32 [2, 256], P('shot'), may hold values from 0 to 1
- wavelet: float32 [4], replicated, may hold values from -4 to 4
- source_x: int32 [256], replicated, may hold values from 0 to 127
- source_y: int32 [256], replicated, may hold values from 0 to 255
- receiver_x: int32 [1024], replicated, may hold values from 0 to 127
- receiver_y: int32 [1024], replicated, may hold values from 0 to 255
Outputs:
- hessian_image: float32 [128, 128, 256], P(('tx', 'ty'), None, 'shot')
- adjoint_first: float32 [2, 128, 256, 128], P('shot', 'tx', 'ty')
- adjoint_second: float32 [2, 128, 256, 128], P('shot', 'tx', 'ty')
- born_last: float32 [2, 128, 256, 128], P('shot', 'tx', 'ty')
- born_before: float32 [2, 128, 256, 128], P('shot', 'tx', 'ty')
The draws below stay inside these ranges and needn't reach their ends.
Inputs may be any that keep to these rules, and one draw needn't show every extreme that they name: `receiver_x`: several receivers may share a cell.
All inputs are finite; a program needn't handle non-finite values.
Results may differ from the reference program's by a relative error of at most 0.00024.
Values sent between devices are 32-bit elements; how exact they have to be, the bound alone decides.
No kernel may reach another device: no remote copies, remote signals or barrier semaphores. Data moves between devices by JAX's collectives and lax.ppermute only.
A program may use at most 128 MiB of HBM per device.

```python
import math
import jax
import jax.numpy as jnp
from jax import lax

NZ = 128
STEPS = 4
NSRC = 256
NREC = 1024
SRC_DEPTH = 4
REC_DEPTH = 2
NSUPER = 2
NX = 128
NY = 256


def with_ends(array, stream_key, smallest, high):
    shape = array.shape
    place = [jax.random.randint(jax.random.fold_in(stream_key, axis), (), 0, shape[axis]) for axis in range(len(shape))]
    array = array.at[tuple(place)].set(smallest)
    longest = shape.index(max(shape))
    place[longest] = (place[longest] + 1) % shape[longest]
    return array.at[tuple(place)].set(high)


def block_levels(own_key, extent, split, low, high):
    loudness = 1.0
    for position, shards_of in split:
        draws = jax.random.uniform(jax.random.fold_in(jax.random.fold_in(own_key, 6), position), (shards_of,), jnp.float32, low / len(split), high / len(split))
        loudness = loudness * jnp.repeat(jnp.exp(draws), extent[position] // shards_of).reshape((-1,) + (1,) * (len(extent) - 1 - position))
    return loudness


def centred(stream_key, dims, spread, bound, split=(), kind=jnp.bfloat16):
    gain = block_levels(stream_key, dims, split, -0.22, 0.18) if split else 1.0
    entries = jax.random.normal(stream_key, dims, jnp.float32) * spread * gain
    return jnp.minimum(jnp.maximum(entries, -bound), bound).astype(kind)


def setup_inputs(seed: int = 0) -> dict:
    keys = jax.random.split(jax.random.key(seed), 15)
    perturbation = centred(keys[0], (NZ, NX, NY), 1.0, 6.0, ((0, 128),), jnp.float32)
    courant_sq = jnp.clip(jnp.exp(math.log(0.3) - 1.3217559 * jax.random.uniform(keys[1], (NX, NY, NZ), jnp.float32) ** block_levels(keys[1], (NX, NY, NZ), ((0, 8), (1, 16)), -0.2, 0.2)), 0.08, 0.3)
    background_prev = centred(keys[2], (NSUPER, NX, NY, NZ), 1.0, 6.0, ((0, 2), (1, 8), (2, 16)), jnp.float32)
    background_now = centred(keys[3], (NSUPER, NX, NY, NZ), 1.0, 6.0, ((0, 2), (1, 8), (2, 16)), jnp.float32)
    born_prev = centred(keys[4], (NSUPER, NX, NY, NZ), 1.0, 6.0, ((0, 2), (1, 8), (2, 16)), jnp.float32)
    born_now = centred(keys[5], (NSUPER, NX, NY, NZ), 1.0, 6.0, ((0, 2), (1, 8), (2, 16)), jnp.float32)
    adjoint_next = centred(keys[6], (NSUPER, NX, NY, NZ), 1.0, 6.0, ((0, 2), (1, 8), (2, 16)), jnp.float32)
    adjoint_after = centred(keys[7], (NSUPER, NX, NY, NZ), 1.0, 6.0, ((0, 2), (1, 8), (2, 16)), jnp.float32)
    encode_bits = with_ends(jax.random.randint(keys[8], (NSUPER, NSRC), 0, 2), jax.random.fold_in(keys[8], 1), 0, 1).astype(jnp.int32)
    wavelet = centred(keys[9], (STEPS,), 1.0, 4.0, (), jnp.float32)
    source_x = with_ends(jax.random.randint(keys[10], (NSRC,), 0, NX), jax.random.fold_in(keys[10], 1), 0, NX - 1).astype(jnp.int32)
    source_y = with_ends(jax.random.randint(keys[11], (NSRC,), 0, NY), jax.random.fold_in(keys[11], 1), 0, NY - 1).astype(jnp.int32)
    receiver_x = with_ends(jax.random.randint(keys[12], (NREC,), 0, NX), jax.random.fold_in(keys[12], 1), 0, NX - 1).astype(jnp.int32)
    receiver_y = with_ends(jax.random.randint(keys[13], (NREC,), 0, NY), jax.random.fold_in(keys[13], 1), 0, NY - 1).astype(jnp.int32)
    return {"perturbation": perturbation, "courant_sq": courant_sq, "background_prev": background_prev, "background_now": background_now, "born_prev": born_prev, "born_now": born_now, "adjoint_next": adjoint_next, "adjoint_after": adjoint_after, "encode_bits": encode_bits, "wavelet": wavelet, "source_x": source_x, "source_y": source_y, "receiver_x": receiver_x, "receiver_y": receiver_y}


def laplace(field):
    padded = jnp.pad(field, ((1, 1), (1, 1), (1, 1)))
    center = padded[1:-1, 1:-1, 1:-1]
    beside = padded[2:, 1:-1, 1:-1] + padded[:-2, 1:-1, 1:-1]
    beside = beside + padded[1:-1, 2:, 1:-1] + padded[1:-1, :-2, 1:-1]
    beside = beside + padded[1:-1, 1:-1, 2:] + padded[1:-1, 1:-1, :-2]
    return beside - 6.0 * center


def reference(perturbation, courant_sq, background_prev, background_now, born_prev, born_now, adjoint_next, adjoint_after, encode_bits, wavelet, source_x, source_y, receiver_x, receiver_y):
    grid_x = jnp.arange(NX, dtype=jnp.int32)
    grid_y = jnp.arange(NY, dtype=jnp.int32)
    depth_index = jnp.arange(NZ, dtype=jnp.int32)
    src_rows = (source_x[:, None] == grid_x[None, :]).astype(jnp.float32)
    src_cols = (source_y[:, None] == grid_y[None, :]).astype(jnp.float32)
    rec_rows = (receiver_x[:, None] == grid_x[None, :]).astype(jnp.float32)
    rec_cols = (receiver_y[:, None] == grid_y[None, :]).astype(jnp.float32)
    rec_plane = jnp.dot(rec_rows.T, rec_cols, precision=lax.Precision.HIGHEST)
    rec_field = rec_plane[:, :, None] * (depth_index == REC_DEPTH).astype(jnp.float32)[None, None, :]
    src_depth = (depth_index == SRC_DEPTH).astype(jnp.float32)
    perturb = perturbation.transpose(1, 2, 0)
    partial_image = jnp.zeros((NX, NY, NZ), jnp.float32)
    firsts = []
    seconds = []
    born_lasts = []
    born_befores = []
    for shot_index in range(NSUPER):
        sign_values = (2 * encode_bits[shot_index] - 1).astype(jnp.float32)
        src_plane = jnp.dot(src_rows.T * sign_values[None, :], src_cols, precision=lax.Precision.HIGHEST)
        src_field = src_plane[:, :, None] * src_depth[None, None, :]
        wave_old = background_prev[shot_index]
        wave_now = background_now[shot_index]
        born_old = born_prev[shot_index]
        born_cur = born_now[shot_index]
        accels = []
        borns = []
        for step_index in range(STEPS):
            accel_now = courant_sq * laplace(wave_now) + wavelet[step_index] * src_field
            wave_new = 2.0 * wave_now - wave_old + accel_now
            born_new = 2.0 * born_cur - born_old + courant_sq * laplace(born_cur) - perturb * accel_now
            accels.append(accel_now)
            borns.append(born_new)
            wave_old, wave_now = wave_now, wave_new
            born_old, born_cur = born_cur, born_new
        born_lasts.append(born_cur)
        born_befores.append(born_old)
        upcoming = adjoint_next[shot_index]
        latest = adjoint_after[shot_index]
        for step_index in range(STEPS, 0, -1):
            current = 2.0 * upcoming - latest + laplace(courant_sq * upcoming) + rec_field * borns[step_index - 1]
            partial_image = partial_image - accels[step_index - 1] * current
            latest, upcoming = upcoming, current
        firsts.append(upcoming)
        seconds.append(latest)
    hessian = partial_image.transpose(2, 0, 1)
    return hessian, jnp.stack(firsts), jnp.stack(seconds), jnp.stack(born_lasts), jnp.stack(born_befores)
```

```python
import functools

import jax
import jax.numpy as jnp
from jax import lax
from jax.experimental import pallas as pl
from jax.experimental.pallas import tpu as pltpu
from jax.sharding import PartitionSpec as P

STEPS = 4
SRC_DEPTH = 4
REC_DEPTH = 2
T = 16
H = 8
E = T + 2 * H
NZ = 128
PAD = 8
WIDTHS = (7, 7, 6, 6, 6, 4, 3)
OFFSETS = tuple(sum(WIDTHS[:i]) for i in range(len(WIDTHS)))
ROWS = sum(WIDTHS)
F32 = jnp.float32
VMEM = pl.BlockSpec(memory_space=pltpu.VMEM)
SMEM = pl.BlockSpec(memory_space=pltpu.SMEM)


def call(body, outs, specs, scratch=(), mib=40):
    return pl.pallas_call(
        body,
        out_shape=outs,
        in_specs=specs,
        out_specs=jax.tree.map(lambda _: VMEM, outs),
        scratch_shapes=list(scratch),
        compiler_params=pltpu.CompilerParams(vmem_limit_bytes=mib * 1024 * 1024),
    )


def lanes(shape):
    return lax.broadcasted_iota(jnp.int32, shape, len(shape) - 1)


def pack_windows(plane_ref, out_ref):
    lane = lanes((8, 128))
    zero = jnp.zeros((8, 128), F32)
    rolled = {}

    def turned(tile, half, amount):
        key = (tile, half, amount)
        if key not in rolled:
            piece = plane_ref[0, 8 * tile : 8 * tile + 8, 128 * half : 128 * half + 128]
            rolled[key] = pltpu.roll(piece, amount, 1) if amount else piece
        return rolled[key]

    for tx in range(8):
        for ty in range(16):
            start = 16 * ty - 8
            block = zero
            for g in range(4):
                tile = 2 * tx - 1 + g
                if tile < 0 or tile > 15:
                    continue
                amount = (32 * g - start) % 128
                for half in range(2):
                    lo = max(start, 128 * half)
                    hi = min(start + 32, 128 * half + 128)
                    if lo >= hi:
                        continue
                    a = 32 * g + lo - start
                    b = 32 * g + hi - start
                    block = jnp.where((lane >= a) & (lane < b), turned(tile, half, amount), block)
            out_ref[16 * tx + ty] = block
        rolled.clear()


def pack_y(par_ref, u0, b0, u1, b1, c, m5, m6, e_ref, o_ref):
    odd = par_ref[1] == 1
    for f, ref in enumerate((u0, b0, u1, b1, c)):
        low = ref[:, 0:8, :]
        high = ref[:, 8:16, :]
        e_ref[f] = jnp.where(odd, low, high)
        o_ref[f] = jnp.where(odd, high, low)
    for f, ref in enumerate((m5, m6)):
        low = ref[:, 0:4, :]
        high = ref[:, 12:16, :]
        e_ref[5, :, 4 * f : 4 * f + 4, :] = jnp.where(odd, low, high)
        o_ref[5, :, 4 * f : 4 * f + 4, :] = jnp.where(odd, high, low)


def pack_x(par_ref, u0, b0, u1, b1, c, m5, m6, ye, yo, e_ref, o_ref):
    odd_x = par_ref[0]
    odd_y = par_ref[1] == 1
    for f, ref in enumerate((u0, b0, u1, b1, c, m5, m6)):
        width = WIDTHS[f]
        for side, out in ((0, e_ref), (1, o_ref)):
            low = odd_x if side == 0 else 1 - odd_x
            first = (1 - low) * (T - width)
            rows = pl.ds(first, width)
            mine = pl.ds(OFFSETS[f], width)
            out[mine, 8:24, :] = ref[rows]
            if f < 5:
                got_e = ye[f, rows]
                got_o = yo[f, rows]
                out[mine, 0:8, :] = jnp.where(odd_y, got_e, got_o)
                out[mine, 24:32, :] = jnp.where(odd_y, got_o, got_e)
            else:
                k = 4 * (f - 5)
                got_e = ye[5, rows, k : k + 4, :]
                got_o = yo[5, rows, k : k + 4, :]
                zero = jnp.zeros((width, 4, NZ), F32)
                out[mine, 0:4, :] = zero
                out[mine, 28:32, :] = zero
                out[mine, 4:8, :] = jnp.where(odd_y, got_e, got_o)
                out[mine, 24:28, :] = jnp.where(odd_y, got_o, got_e)


def count_planes(first_ref, sx, sy, bits, rx, ry, src_ref, rec_ref):
    def one_hot(values, start, rows):
        grid = lax.broadcasted_iota(jnp.int32, (rows, values.shape[1]), 0) + start
        return jnp.where(grid == values, 1.0, 0.0).astype(F32)

    x0 = first_ref[0]
    y0 = first_ref[1]
    dims = (((1,), (1,)), ((), ()))
    sign = (2 * bits[...] - 1).astype(F32)
    src_ref[...] = lax.dot_general(
        one_hot(sy[...], y0, E), one_hot(sx[...], x0, 128) * sign, dims, preferred_element_type=F32
    )
    rec_ref[...] = lax.dot_general(
        one_hot(ry[...], y0, E), one_hot(rx[...], x0, 128), dims, preferred_element_type=F32
    )


def propagate(
    par_ref, wavelet, u0, b0, u1, b1, c, m5, m6, ye, yo, xe, xo, pert, src, rec,
    image, first, second, last, before,
    U0, U1, B, C, M0, M1, Q0, Q1, PT, SF, RF, A,
):
    odd_x = par_ref[0] == 1
    odd_y = par_ref[1] == 1
    lane = lanes((1, 1, NZ))
    own_y = pl.ds(PAD + H, T)
    all_y = pl.ds(PAD, E)

    with jax.named_scope("assemble"):
        targets = (U0, B.at[1], U1, B.at[0], C, M0, M1)
        for f, (ref, ext) in enumerate(zip((u0, b0, u1, b1, c, m5, m6), targets)):
            ext[H : H + T, own_y, :] = ref[...]
            if f < 5:
                ext[H : H + T, PAD : PAD + 8, :] = jnp.where(odd_y, ye[f], yo[f])
                ext[H : H + T, PAD + 24 : PAD + 32, :] = jnp.where(odd_y, yo[f], ye[f])
            else:
                k = 4 * (f - 5)
                got_e = ye[5, :, k : k + 4, :]
                got_o = yo[5, :, k : k + 4, :]
                ext[H : H + T, PAD + 4 : PAD + 8, :] = jnp.where(odd_y, got_e, got_o)
                ext[H : H + T, PAD + 24 : PAD + 28, :] = jnp.where(odd_y, got_o, got_e)
            width = WIDTHS[f]
            rows = pl.ds(OFFSETS[f], width)
            got_e = xe[rows]
            got_o = xo[rows]
            ext[H - width : H, all_y, :] = jnp.where(odd_x, got_e, got_o)
            ext[H + T : H + T + width, all_y, :] = jnp.where(odd_x, got_o, got_e)
        for s in range(8):
            turned = pert[:, s, :].T
            for g in range(4):
                PT[8 * g + s] = turned[32 * g : 32 * g + 32, :]
        plane = src[...]
        counts = rec[...]
        lane2 = lanes((E, NZ))
        for x in range(E):
            SF[x] = jnp.where(lane2 == SRC_DEPTH, pltpu.roll(plane, (SRC_DEPTH - x) % NZ, 1), 0.0)
            RF[x] = jnp.where(lane2 == REC_DEPTH, pltpu.roll(counts, (REC_DEPTH - x) % NZ, 1), 0.0)

    def laplace(ref, x, n, ys, ny):
        rows = pl.ds(x, n)
        center = ref[rows, pl.ds(ys, ny), :]
        total = ref[pl.ds(x + 1, n), pl.ds(ys, ny), :] + ref[pl.ds(x - 1, n), pl.ds(ys, ny), :]
        total = total + ref[rows, pl.ds(ys + 1, ny), :] + ref[rows, pl.ds(ys - 1, ny), :]
        down = jnp.where(lane == NZ - 1, 0.0, pltpu.roll(center, NZ - 1, 2))
        up = jnp.where(lane == 0, 0.0, pltpu.roll(center, 1, 2))
        return center, total + down + up - 6.0 * center

    def loop(start, blocks, n, body):
        def step(i, carry):
            body(start + i * n)
            return carry

        lax.fori_loop(0, blocks, step, 0)

    N = 4
    waves = (U1, U0)
    for t in range(STEPS):
        with jax.named_scope("forward"):
            old, now = waves
            b_old, b_now, b_new = B.at[t], B.at[t + 1], B.at[t + 2]
            scale = wavelet[t]

            def forward(x):
                rows = pl.ds(x, N)
                speed = C[rows, all_y, :]
                center, lap = laplace(now, x, N, PAD, E)
                accel = speed * lap + scale * SF[rows]
                A[t, rows] = accel
                old[rows, all_y, :] = 2.0 * center - old[rows, all_y, :] + accel
                center, lap = laplace(b_now, x, N, PAD, E)
                b_new[rows, all_y, :] = (
                    2.0 * center - b_old[rows, all_y, :] + speed * lap - PT[rows] * accel
                )

            begin, blocks = ((2, 7), (2, 7), (4, 6), (4, 6))[t]
            loop(begin, blocks, N, forward)
            waves = (now, old)

    def scaled(x):
        rows = pl.ds(x, N)
        Q0[rows, all_y, :] = C[rows, all_y, :] * M0[rows, all_y, :]

    loop(4, 6, N, scaled)
    upcoming, latest, q_now, q_new = M0, M1, Q0, Q1
    for t in range(STEPS, 1, -1):
        with jax.named_scope("adjoint"):
            def back(x):
                rows = pl.ds(x, N)
                _, lap = laplace(q_now, x, N, PAD, E)
                current = 2.0 * upcoming[rows, all_y, :] - latest[rows, all_y, :] + lap
                current = current + RF[rows] * B[t + 1, rows, all_y, :]
                latest[rows, all_y, :] = current
                q_new[rows, all_y, :] = C[rows, all_y, :] * current

            begin, blocks = {4: (4, 6), 3: (6, 5), 2: (6, 5)}[t]
            loop(begin, blocks, N, back)
            upcoming, latest = latest, upcoming
            q_now, q_new = q_new, q_now

            def imaging(x):
                rows = pl.ds(x + H, N)
                product = A[t - 1, rows, H : H + T, :] * upcoming[rows, own_y, :]
                if t == STEPS:
                    SF[rows, 0:T, :] = -product
                else:
                    SF[rows, 0:T, :] = SF[rows, 0:T, :] - product

            loop(0, 4, N, imaging)

    with jax.named_scope("final"):
        def finish(x):
            rows = pl.ds(x + H, N)
            mine = pl.ds(x, N)
            _, lap = laplace(q_now, x + H, N, PAD + H, T)
            current = 2.0 * upcoming[rows, own_y, :] - latest[rows, own_y, :] + lap
            current = current + RF[rows, H : H + T, :] * B[2, rows, own_y, :]
            first[mine] = current
            second[mine] = upcoming[rows, own_y, :]
            last[mine] = B[5, rows, own_y, :]
            before[mine] = B[4, rows, own_y, :]
            SF[rows, 0:T, :] = SF[rows, 0:T, :] - A[0, rows, H : H + T, :] * current

        loop(0, 4, N, finish)
        for half in range(2):
            part = SF[H + 8 * half : H + 8 * half + 8, 0:T, :].reshape(128, NZ)
            image[pl.ds(half, 128, stride=2), :] = part.T


def sum_shots(arrived, out):
    for tx in range(8):
        out[16 * tx : 16 * tx + 16, :] = arrived[32 * tx : 32 * tx + 16, :] + arrived[32 * tx + 16 : 32 * tx + 32, :]


def arrange(keep_ref, mine, other, out):
    keep = keep_ref[0] == 1
    lane = lanes((8, NZ))
    for half in range(2):
        groups = []
        for j in range(8):
            rows = pl.ds(2 * j + half, 8, stride=16)
            groups.append(jnp.where(keep, mine[rows, :], other[rows, :]))
        for k in range(8):
            line = jnp.zeros((8, NZ), F32)
            for j in range(8):
                amount = (16 * j - 16 * k) % NZ
                piece = pltpu.roll(groups[j], amount, 1) if amount else groups[j]
                line = jnp.where((lane >= 16 * j) & (lane < 16 * j + 16), piece, line)
            out[pl.ds(8 * half + k, 8, stride=16), :] = line


def swap(cells, axis, odd):
    count = lax.axis_size(axis)
    pairs = [(i, ((i - odd) ^ 1) + odd) for i in range(odd, count - odd)]
    return lax.ppermute(cells, axis, pairs)


def image_groups():
    groups = []
    for h in range(2):
        members = []
        for z in range(128):
            tx, ty = z // 16, z % 16
            members.append(h * 128 + z if ty // 8 == h else (1 - h) * 128 + tx * 16 + (ty ^ 8))
        groups.append(members)
    return groups


def per_device(
    perturbation, courant_sq, background_prev, background_now, born_prev, born_now,
    adjoint_next, adjoint_after, encode_bits, wavelet, source_x, source_y, receiver_x, receiver_y,
):
    shape = jax.ShapeDtypeStruct
    tile = (T, T, NZ)
    shot, tx, ty = lax.axis_index("shot"), lax.axis_index("tx"), lax.axis_index("ty")
    parity = jnp.stack([tx % 2, ty % 2]).astype(jnp.int32)
    corner = jnp.stack([tx * T - H, ty * T - H]).astype(jnp.int32)
    fields = [
        a.reshape(tile)
        for a in (background_now, born_now, background_prev, born_prev, courant_sq, adjoint_next, adjoint_after)
    ]

    blocks = call(pack_windows, shape((128, 8, 128), F32), [VMEM])(perturbation)
    strip = shape((6, T, 8, NZ), F32)
    send_e, send_o = call(pack_y, (strip, strip), [SMEM] + [VMEM] * 7)(parity, *fields)
    got_ye = swap(send_e, "ty", 0)
    got_yo = swap(send_o, "ty", 1)
    windows = lax.all_to_all(blocks, ("tx", "ty"), split_axis=0, concat_axis=0, tiled=True)
    strip = shape((ROWS, E, NZ), F32)
    send_e, send_o = call(pack_x, (strip, strip), [SMEM] + [VMEM] * 9)(parity, *fields, got_ye, got_yo)
    got_xe = swap(send_e, "tx", 0)
    got_xo = swap(send_o, "tx", 1)

    counts = shape((E, 128), F32)
    src, rec = call(count_planes, (counts, counts), [SMEM] + [VMEM] * 5)(
        corner, source_x[None], source_y[None], encode_bits, receiver_x[None], receiver_y[None]
    )

    wide = pltpu.VMEM((E, E + 2 * PAD, NZ), F32)
    flat = pltpu.VMEM((E, E, NZ), F32)
    many = pltpu.VMEM((STEPS + 2, E, E + 2 * PAD, NZ), F32)
    out = shape(tile, F32)
    image, first, second, last, before = call(
        propagate,
        (shape((256, NZ), F32), out, out, out, out),
        [SMEM, SMEM] + [VMEM] * 14,
        (wide, wide, many, wide, wide, wide, wide, wide, flat, flat, flat, pltpu.VMEM((STEPS, E, E, NZ), F32)),
    )(parity, wavelet, *fields, got_ye, got_yo, got_xe, got_xo, windows, src, rec)

    arrived = lax.all_to_all(
        image.reshape(128, 2, NZ), ("shot", "tx", "ty"), split_axis=0, concat_axis=0, tiled=True,
        axis_index_groups=image_groups(),
    )
    summed = call(sum_shots, shape((128, NZ), F32), [VMEM])(arrived.reshape(256, NZ))
    pairs = [(16 + y, 8 + y) for y in range(8)] + [(8 + y, 16 + y) for y in range(8)]
    other = lax.ppermute(summed, ("shot", "ty"), pairs)
    keep = jnp.where(ty // 8 == shot, 1, 0).astype(jnp.int32)[None]
    hessian = call(arrange, shape((128, NZ), F32), [SMEM, VMEM, VMEM])(keep, summed, other)
    fit = lambda a: a[None]
    return (hessian[None], fit(first), fit(second), fit(last), fit(before))


def solution(mesh):
    field = P("shot", "tx", "ty", None)
    placed = (
        P(("tx", "ty"), None, None),
        P("tx", "ty", None),
        field, field, field, field, field, field,
        P("shot", None),
        P(), P(), P(), P(), P(),
    )
    return jax.shard_map(
        per_device,
        mesh=mesh,
        in_specs=placed,
        out_specs=(P(("tx", "ty"), None, "shot"), field, field, field, field),
        check_vma=False,
    )
```

```python
import jax
import jax.numpy as jnp
from jax import lax
from jax.experimental import pallas as pl
from jax.experimental.pallas import tpu as pltpu
from jax.sharding import PartitionSpec as P

STEPS = 4
SRC_DEPTH = 4
REC_DEPTH = 2
NZ = 128
T = 16
D = 4
G = T + 2 * D
H = 8
E = T + 2 * H
PAD = 8
XO = 1
SH = 8
WIDTHS = (4, 4, 4, 4, 3, 3, 3)
OFFSETS = tuple(sum(WIDTHS[:i]) * G for i in range(len(WIDTHS)))
SHALLOW = (0, 1, 2, 4, 5)
SHALLOW_ROW = sum(WIDTHS) * G
STRIP_Y = (4 * T + len(SHALLOW), 8, NZ)
STRIP_X = (SHALLOW_ROW + len(SHALLOW) * E, NZ)
F32 = jnp.float32
VMEM = pl.BlockSpec(memory_space=pltpu.VMEM)
SMEM = pl.BlockSpec(memory_space=pltpu.SMEM)
HBM = pl.BlockSpec(memory_space=pltpu.HBM)


def call(body, outs, specs, scratch=(), mib=32, cost=None):
    return pl.pallas_call(
        body,
        out_shape=outs,
        in_specs=specs,
        out_specs=jax.tree.map(lambda _: VMEM, outs),
        scratch_shapes=list(scratch),
        compiler_params=pltpu.CompilerParams(vmem_limit_bytes=mib and mib * 1024 * 1024),
        cost_estimate=cost,
    )


def lanes(shape):
    return lax.broadcasted_iota(jnp.int32, shape, len(shape) - 1)


def turn(piece, amount):
    amount = amount % NZ
    return pltpu.roll(piece, amount, len(piece.shape) - 1) if amount else piece


def pack_windows(plane_ref, out_ref):
    lane = lanes((8, 128))
    zero = jnp.zeros((8, 128), F32)
    turned = {}

    def piece(tile, half, amount):
        key = (tile, half, amount % NZ)
        if key not in turned:
            turned[key] = turn(plane_ref[0, 8 * tile : 8 * tile + 8, 128 * half : 128 * half + 128], amount)
        return turned[key]

    for tx in range(8):
        for ty in range(16):
            start = 16 * ty - 8
            block = zero
            for g in range(4):
                tile = 2 * tx - 1 + g
                if tile < 0 or tile > 15:
                    continue
                for half in range(2):
                    lo = max(start, 128 * half)
                    hi = min(start + 32, 128 * half + 128)
                    if lo >= hi:
                        continue
                    a = 32 * g + lo - start
                    b = 32 * g + hi - start
                    block = jnp.where((lane >= a) & (lane < b), piece(tile, half, 32 * g - start), block)
            out_ref[16 * tx + ty] = block
        turned.clear()


def pack_y(par_ref, *refs):
    sources, refs = refs[:7], refs[7:]
    e_ref, o_ref, shallow, fields, sems = refs[0], refs[1], refs[2], refs[3:10], refs[10]
    copies = [
        pltpu.make_async_copy(source, field, sems.at[f])
        for f, (source, field) in enumerate(zip(sources, fields))
    ]
    for copy in copies:
        copy.start()
    odd = par_ref[1] == 1
    lane = lanes((T, NZ))
    for f, ref in enumerate(fields):
        copies[f].wait()
        slot, k = f // 2, 4 * (f % 2)
        low = ref[:, 0:4, :]
        high = ref[:, 12:16, :]
        e_ref[T * slot : T * slot + T, k : k + 4, :] = jnp.where(odd, low, high)
        o_ref[T * slot : T * slot + T, k : k + 4, :] = jnp.where(odd, high, low)
        if f in SHALLOW:
            i = SHALLOW.index(f)
            packed = ref[0]
            for x in range(1, T):
                packed = jnp.where(lane >= SH * x, turn(ref[x], SH * x), packed)
            shallow[T * i : T * i + T, :] = packed
            e_ref[4 * T + i] = jnp.where(odd, packed[0:8], packed[8:16])
            o_ref[4 * T + i] = jnp.where(odd, packed[8:16], packed[0:8])
    e_ref[3 * T : 4 * T, 4:8, :] = jnp.zeros((T, 4, NZ), F32)
    o_ref[3 * T : 4 * T, 4:8, :] = jnp.zeros((T, 4, NZ), F32)


def pack_x(par_ref, *refs):
    fields, (shallow, ye, yo, e_ref, o_ref) = refs[:7], refs[7:]
    odd_x = par_ref[0]
    odd_y = par_ref[1] == 1
    for f, ref in enumerate(fields):
        width = WIDTHS[f]
        slot, k = f // 2, 4 * (f % 2)
        for low, out in ((odd_x, e_ref), (1 - odd_x, o_ref)):
            first = (1 - low) * (T - width)
            for i in range(width):
                x = first + i
                row = OFFSETS[f] + G * i
                got_e = ye[T * slot + x, k : k + 4, :]
                got_o = yo[T * slot + x, k : k + 4, :]
                out[row : row + 4, :] = jnp.where(odd_y, got_e, got_o)
                out[row + 4 : row + 20, :] = ref[x]
                out[row + 20 : row + 24, :] = jnp.where(odd_y, got_o, got_e)
    for i in range(len(SHALLOW)):
        row = SHALLOW_ROW + E * i
        got_e = ye[4 * T + i]
        got_o = yo[4 * T + i]
        for out in (e_ref, o_ref):
            out[row : row + 8, :] = jnp.where(odd_y, got_e, got_o)
            out[row + 8 : row + 24, :] = shallow[T * i : T * i + T, :]
            out[row + 24 : row + 32, :] = jnp.where(odd_y, got_o, got_e)


def count_planes(first_ref, sx, sy, bits, rx, ry, src_ref, rec_ref):
    x0 = first_ref[0] - T
    y0 = first_ref[1] - H

    def rows(values):
        grid = lax.broadcasted_iota(jnp.int32, (E, values.shape[1]), 0) + y0
        return jnp.where(grid == values, 1.0, 0.0).astype(F32)

    dims = (((1,), (1,)), ((), ()))
    sign = (2 * bits[...] - 1).astype(F32)
    for values, ys, depth, weight, out in (
        (sx[...], sy[...], SRC_DEPTH, sign, src_ref),
        (rx[...], ry[...], REC_DEPTH, None, rec_ref),
    ):
        left = rows(ys)
        if weight is not None:
            left = left * weight
        grid = lax.broadcasted_iota(jnp.int32, (NZ, values.shape[1]), 0)
        here = grid % SH == depth
        for piece in range(3):
            hit = here & (grid // SH + (x0 + T * piece) == values)
            right = jnp.where(hit, 1.0, 0.0).astype(F32)
            out[piece] = lax.dot_general(left, right, dims, preferred_element_type=F32)


def propagate(par_ref, wavelet, *refs):
    fields, refs = refs[:7], refs[7:]
    shallow, ye, yo, xe, xo, pert, src, rec = refs[:8]
    image, first, second, last, before = refs[8:13]
    U0, U1, B, C, M0, M1, Q0, Q1, PT, SF, A, IN, IM, US, BS, CS, PS = refs[13:]
    odd_x = par_ref[0] == 1
    odd_y = par_ref[1] == 1
    lane = lanes((1, 1, NZ))
    all_y = pl.ds(PAD, G)
    own_y = pl.ds(PAD + D, T)
    own_x = pl.ds(XO + D, T)

    def pick(test, a, b):
        return jnp.where(test, a, b)

    with jax.named_scope("assemble"):
        targets = (U0, B.at[1], C, M0, U1, B.at[0], M1)
        for f, (ref, ext) in enumerate(zip(fields, targets)):
            slot, k = f // 2, 4 * (f % 2)
            ext[own_x, own_y, :] = ref[...]
            got_e = ye[T * slot : T * slot + T, k : k + 4, :]
            got_o = yo[T * slot : T * slot + T, k : k + 4, :]
            ext[own_x, PAD : PAD + 4, :] = pick(odd_y, got_e, got_o)
            ext[own_x, PAD + 20 : PAD + 24, :] = pick(odd_y, got_o, got_e)
            width = WIDTHS[f]
            for i in range(width):
                rows = pl.ds(OFFSETS[f] + G * i, G)
                got_e = xe[rows, :]
                got_o = xo[rows, :]
                ext[XO + D - width + i, all_y, :] = pick(odd_x, got_e, got_o)
                ext[XO + D + T + i, all_y, :] = pick(odd_x, got_o, got_e)
        targets = (US.at[0], BS.at[1], CS, US.at[1], BS.at[0])
        blank = jnp.zeros((3, PAD, NZ), F32)
        for a in (US.at[0], US.at[1], *(BS.at[i] for i in range(STEPS + 2))):
            a[:, 0:PAD, :] = blank
            a[:, PAD + E : PAD + E + PAD, :] = blank
        for i, ext in enumerate(targets):
            rows = pl.ds(SHALLOW_ROW + E * i, E)
            got_e = xe[rows, :]
            got_o = xo[rows, :]
            ext[0, PAD : PAD + E, :] = pick(odd_x, got_e, got_o)
            ext[2, PAD : PAD + E, :] = pick(odd_x, got_o, got_e)
            ext[1, PAD + H : PAD + H + T, :] = shallow[T * i : T * i + T, :]
            got_e = ye[4 * T + i]
            got_o = yo[4 * T + i]
            ext[1, PAD : PAD + H, :] = pick(odd_y, got_e, got_o)
            ext[1, PAD + H + T : PAD + E, :] = pick(odd_y, got_o, got_e)
        for s in range(8):
            turned = pert[:, s, :].T
            for g in range(4):
                PT[8 * g + s] = turned[32 * g : 32 * g + 32, :]
        flat = lanes((E, NZ))
        for piece, (lo, hi) in enumerate(((-7, 0), (0, 16), (16, 23))):
            packed = jnp.zeros((E, NZ), F32)
            for x in range(lo, hi):
                at = SH * (x % T)
                packed = jnp.where((flat >= at) & (flat < at + SH), turn(PT[x + H], at), packed)
            PS[piece] = packed
        short = lanes((G, NZ))
        for x in range(1, G - 1):
            piece, at = (x - D + T) // T, SH * ((x - D) % T)
            SF[XO + x] = jnp.where(short == SRC_DEPTH, turn(src[piece, 4:28, :], -at), 0.0)

    with jax.named_scope("shallow"):
        rows = pl.ds(PAD, E)
        narrow = lanes((3, E, NZ))

        def shallow_laplace(ref):
            center = ref[:, rows, :]
            total = ref[:, pl.ds(PAD + 1, E), :] + ref[:, pl.ds(PAD - 1, E), :]
            total = total + jnp.where(narrow % SH == SH - 1, 0.0, turn(center, -1))
            total = total + jnp.where(narrow % SH == 0, 0.0, turn(center, 1))
            left = turn(center, SH)
            right = turn(center, -SH)
            none = jnp.zeros((1, E, NZ), F32)
            left = jnp.where(narrow < SH, jnp.concatenate([none, left[0:2]], 0), left)
            right = jnp.where(narrow >= NZ - SH, jnp.concatenate([right[1:3], none], 0), right)
            return center, total + left + right - 6.0 * center

        speed = CS[:, rows, :]
        for t in range(STEPS):
            now, old = US.at[t % 2], US.at[1 - t % 2]
            center, lap = shallow_laplace(now)
            accel = speed * lap + wavelet[t] * src[...]
            if t < STEPS - 1:
                old[:, rows, :] = 2.0 * center - old[:, rows, :] + accel
            center, lap = shallow_laplace(BS.at[t + 1])
            BS[t + 2, :, rows, :] = 2.0 * center - BS[t, :, rows, :] + speed * lap - PS[...] * accel
        for t in range(1, STEPS + 1):
            BS[t + 1, :, rows, :] = rec[...] * BS[t + 1, :, rows, :]
            for x in range(D + 1 - t, G - D - 1 + t):
                piece, at = (x - D + T) // T, SH * ((x - D) % T)
                IN[t - 1, XO + x] = jnp.where(
                    short == REC_DEPTH, turn(BS[t + 1, piece, PAD + 4 : PAD + 28, :], -at), 0.0
                )

    def laplace(ref, x, n, ys, ny):
        rows = pl.ds(x, n)
        center = ref[rows, pl.ds(ys, ny), :]
        total = ref[pl.ds(x + 1, n), pl.ds(ys, ny), :] + ref[pl.ds(x - 1, n), pl.ds(ys, ny), :]
        total = total + ref[rows, pl.ds(ys + 1, ny), :] + ref[rows, pl.ds(ys - 1, ny), :]
        down = jnp.where(lane == NZ - 1, 0.0, turn(center, -1))
        up = jnp.where(lane == 0, 0.0, turn(center, 1))
        return center, total + down + up - 6.0 * center

    def loop(start, blocks, n, body):
        def step(i, carry):
            body(XO + start + i * n)
            return carry

        lax.fori_loop(0, blocks, step, 0)

    waves = (U1, U0)
    plan = ((0, 4, 6), (2, 5, 4), (3, 3, 6), (4, 4, 4))
    for t in range(STEPS):
        with jax.named_scope("forward"):
            old, now = waves
            b_old, b_now, b_new = B.at[t], B.at[t + 1], B.at[t + 2]
            scale = wavelet[t]
            start, blocks, n = plan[t]

            def forward(x):
                rows = pl.ds(x, n)
                speed = C[rows, all_y, :]
                center, lap = laplace(now, x, n, PAD, G)
                accel = speed * lap + scale * SF[rows]
                A[t, rows] = accel
                if t < STEPS - 1:
                    old[rows, all_y, :] = 2.0 * center - old[rows, all_y, :] + accel
                center, lap = laplace(b_now, x, n, PAD, G)
                b_new[rows, all_y, :] = (
                    2.0 * center - b_old[rows, all_y, :] + speed * lap
                    - PT[pl.ds(x - XO + 4, n), 4:28, :] * accel
                )

            loop(start, blocks, n, forward)
            waves = (now, old)

    def scaled(x):
        rows = pl.ds(x, 6)
        Q0[rows, all_y, :] = C[rows, all_y, :] * M0[rows, all_y, :]

    loop(0, 4, 6, scaled)
    upcoming, latest, q_now, q_new = M0, M1, Q0, Q1
    for t in range(STEPS, 1, -1):
        with jax.named_scope("adjoint"):
            start, blocks, n = plan[STEPS - t]

            def back(x):
                rows = pl.ds(x, n)
                _, lap = laplace(q_now, x, n, PAD, G)
                current = 2.0 * upcoming[rows, all_y, :] - latest[rows, all_y, :] + lap + IN[t - 1, rows]
                latest[rows, all_y, :] = current
                q_new[rows, all_y, :] = C[rows, all_y, :] * current

            loop(start, blocks, n, back)
            upcoming, latest = latest, upcoming
            q_now, q_new = q_new, q_now

            def imaging(x):
                rows = pl.ds(x, 4)
                product = A[t - 1, rows] * upcoming[rows, all_y, :]
                IM[rows] = -product if t == STEPS else IM[rows] - product

            loop(D, 4, 4, imaging)

    with jax.named_scope("final"):
        def finish(x):
            rows = pl.ds(x, 4)
            mine = pl.ds(x - XO - D, 4)
            _, lap = laplace(q_now, x, 4, PAD + D, T)
            current = 2.0 * upcoming[rows, own_y, :] - latest[rows, own_y, :] + lap
            current = current + IN[0, rows, D : D + T, :]
            first[mine] = current
            second[mine] = upcoming[rows, own_y, :]
            last[mine] = B[5, rows, own_y, :]
            before[mine] = B[4, rows, own_y, :]
            IM[rows, D : D + T, :] = IM[rows, D : D + T, :] - A[0, rows, D : D + T, :] * current

        loop(D, 4, 4, finish)
        for half in range(2):
            rows = pl.ds(XO + D + 8 * half, 8)
            turned = IM[rows, D : D + T, :].reshape(128, NZ).T
            for shot in range(2):
                image[pl.ds(256 * shot + half, 128, stride=2), :] = turned


def arrange(shot_ref, arrived, out):
    first = shot_ref[0] * 16
    lane = lanes((8, NZ))
    for half in range(2):
        groups = []
        for j in range(8):
            groups.append(
                arrived[pl.ds(first + 2 * j + half, 8, stride=32), :]
                + arrived[pl.ds(first + 256 + 2 * j + half, 8, stride=32), :]
            )
        for k in range(8):
            line = jnp.zeros((8, NZ), F32)
            for j in range(8):
                line = jnp.where((lane >= 16 * j) & (lane < 16 * j + 16), turn(groups[j], 16 * j - 16 * k), line)
            out[pl.ds(8 * half + k, 8, stride=16), :] = line


def swap(cells, axis, odd):
    count = lax.axis_size(axis)
    pairs = [(i, ((i - odd) ^ 1) + odd) for i in range(odd, count - odd)]
    return lax.ppermute(cells, axis, pairs)


def per_device(
    perturbation, courant_sq, background_prev, background_now, born_prev, born_now,
    adjoint_next, adjoint_after, encode_bits, wavelet, source_x, source_y, receiver_x, receiver_y,
):
    shape = lambda *dims: jax.ShapeDtypeStruct(dims, F32)
    tile = (T, T, NZ)
    shot, tx, ty = lax.axis_index("shot"), lax.axis_index("tx"), lax.axis_index("ty")
    parity = jnp.stack([tx % 2, ty % 2]).astype(jnp.int32)
    corner = jnp.stack([tx * T, ty * T]).astype(jnp.int32)
    fields = [
        a.reshape(tile)
        for a in (background_now, born_now, courant_sq, adjoint_next, background_prev, born_prev, adjoint_after)
    ]

    send_e, send_o, shallow = call(
        pack_y,
        (shape(*STRIP_Y), shape(*STRIP_Y), shape(5 * T, NZ)),
        [SMEM] + [HBM] * 7,
        [pltpu.VMEM(tile, F32)] * 7 + [pltpu.SemaphoreType.DMA((7,))],
        mib=None,
    )(parity, *fields)
    got_ye = swap(send_e, "ty", 0)
    got_yo = swap(send_o, "ty", 1)
    blocks = call(pack_windows, shape(128, 8, 128), [VMEM])(perturbation)
    windows = lax.all_to_all(blocks, ("tx", "ty"), split_axis=0, concat_axis=0, tiled=True)
    send_e, send_o = call(
        pack_x,
        (shape(*STRIP_X), shape(*STRIP_X)),
        [SMEM] + [VMEM] * 10,
        cost=pl.CostEstimate(flops=10**15, bytes_accessed=10**9, transcendentals=0),
    )(parity, *fields, shallow, got_ye, got_yo)
    got_xe = swap(send_e, "tx", 0)
    got_xo = swap(send_o, "tx", 1)

    src, rec = call(count_planes, (shape(3, E, NZ), shape(3, E, NZ)), [SMEM] + [VMEM] * 5)(
        corner, source_x[None], source_y[None], encode_bits, receiver_x[None], receiver_y[None]
    )

    wide = pltpu.VMEM((G + 2 * XO, G + 2 * PAD, NZ), F32)
    flat = pltpu.VMEM((G + 2 * XO, G, NZ), F32)
    many = pltpu.VMEM((STEPS + 2, G + 2 * XO, G + 2 * PAD, NZ), F32)
    each = pltpu.VMEM((STEPS, G + 2 * XO, G, NZ), F32)
    low = lambda n: pltpu.VMEM((n, 3, E + 2 * PAD, NZ), F32)
    image, first, second, last, before = call(
        propagate,
        (shape(512, NZ),) + (shape(*tile),) * 4,
        [SMEM, SMEM] + [VMEM] * 15,
        (
            wide, wide, many, wide, wide, wide, wide, wide, pltpu.VMEM((E, E, NZ), F32), flat, each, each, flat,
            low(2), low(STEPS + 2), pltpu.VMEM((3, E + 2 * PAD, NZ), F32), pltpu.VMEM((3, E, NZ), F32),
        ),
    )(parity, wavelet, *fields, shallow, got_ye, got_yo, got_xe, got_xo, windows, src, rec)

    arrived = lax.all_to_all(
        image.reshape(256, 2, NZ), ("shot", "tx", "ty"), split_axis=0, concat_axis=0, tiled=True
    )
    hessian = call(arrange, shape(128, NZ), [SMEM, VMEM])(shot.astype(jnp.int32)[None], arrived.reshape(512, NZ))
    return (hessian[None], first[None], second[None], last[None], before[None])


def solution(mesh):
    field = P("shot", "tx", "ty", None)
    placed = (
        P(("tx", "ty"), None, None),
        P("tx", "ty", None),
        field, field, field, field, field, field,
        P("shot", None),
        P(), P(), P(), P(), P(),
    )
    return jax.shard_map(
        per_device,
        mesh=mesh,
        in_specs=placed,
        out_specs=(P(("tx", "ty"), None, "shot"), field, field, field, field),
        check_vma=False,
    )
```

```python
import jax
import jax.numpy as jnp
from jax import lax
from jax.experimental import pallas as pl
from jax.experimental.pallas import tpu as pltpu
from jax.sharding import PartitionSpec as P

STEPS = 4
SRC_DEPTH = 4
REC_DEPTH = 2
NZ = 128
T = 16
D = 4
G = T + 2 * D
H = 8
E = T + 2 * H
PAD = 8
XO = 1
SH = 8
WIDTHS = (4, 4, 4, 4, 3, 3, 3)
OFFSETS = tuple(sum(WIDTHS[:i]) * G for i in range(len(WIDTHS)))
SHALLOW = (0, 1, 2, 4, 5)
SHALLOW_ROW = sum(WIDTHS) * G
STRIP_Y = (4 * T + 5, 8, NZ)
STRIP_X = (SHALLOW_ROW + len(SHALLOW) * E, NZ)
F32 = jnp.float32
VMEM = pl.BlockSpec(memory_space=pltpu.VMEM)
SMEM = pl.BlockSpec(memory_space=pltpu.SMEM)
HBM = pl.BlockSpec(memory_space=pltpu.HBM)


BUSY = pl.CostEstimate(flops=10**15, bytes_accessed=10**9, transcendentals=0)


def call(body, outs, specs, scratch=(), mib=32, cost=None):
    return pl.pallas_call(
        body,
        out_shape=outs,
        in_specs=specs,
        out_specs=jax.tree.map(lambda _: VMEM, outs),
        scratch_shapes=list(scratch),
        compiler_params=pltpu.CompilerParams(vmem_limit_bytes=mib and mib * 1024 * 1024),
        cost_estimate=cost,
    )


def lanes(shape):
    return lax.broadcasted_iota(jnp.int32, shape, len(shape) - 1)


def turn(piece, amount):
    amount = amount % NZ
    return pltpu.roll(piece, amount, len(piece.shape) - 1) if amount else piece


def pack_windows(plane_ref, out_ref):
    lane = lanes((8, 128))
    zero = jnp.zeros((8, 128), F32)
    turned = {}

    def piece(tile, half, amount):
        key = (tile, half, amount % NZ)
        if key not in turned:
            turned[key] = turn(plane_ref[8 * tile : 8 * tile + 8, 128 * half : 128 * half + 128], amount)
        return turned[key]

    for tx in range(8):
        for ty in range(16):
            start = 16 * ty - 8
            block = zero
            for g in range(4):
                tile = 2 * tx - 1 + g
                if tile < 0 or tile > 15:
                    continue
                for half in range(2):
                    lo = max(start, 128 * half)
                    hi = min(start + 32, 128 * half + 128)
                    if lo >= hi:
                        continue
                    a = 32 * g + lo - start
                    b = 32 * g + hi - start
                    block = jnp.where((lane >= a) & (lane < b), piece(tile, half, 32 * g - start), block)
            out_ref[16 * tx + ty] = block
        turned.clear()


def parity():
    return lax.rem(lax.axis_index("tx"), 2), lax.rem(lax.axis_index("ty"), 2)


def strips(ref, e_ref, o_ref, row, k):
    odd = parity()[1] == 1
    low = ref[:, 0:4, :]
    high = ref[:, 12:16, :]
    e_ref[row : row + T, k : k + 4, :] = jnp.where(odd, low, high)
    o_ref[row : row + T, k : k + 4, :] = jnp.where(odd, high, low)


def shallow_strips(ref, e_ref, o_ref, row, shallow, at):
    odd = parity()[1] == 1
    lane = lanes((T, NZ))
    packed = ref[0]
    for x in range(1, T):
        packed = jnp.where(lane >= SH * x, turn(ref[x], SH * x), packed)
    shallow[at : at + T, :] = packed
    e_ref[row] = jnp.where(odd, packed[0:8], packed[8:16])
    o_ref[row] = jnp.where(odd, packed[8:16], packed[0:8])


def pack_fields(*refs):
    sources, (e_ref, o_ref, shallow), targets, sems = refs[:8], refs[8:11], refs[11:19], refs[19]
    copies = [pltpu.make_async_copy(a, b, sems.at[i]) for i, (a, b) in enumerate(zip(sources, targets))]
    for copy in copies:
        copy.start()
    for f, ref in enumerate(targets[:7]):
        copies[f].wait()
        strips(ref, e_ref, o_ref, T * (f // 2), 4 * (f % 2))
        if f in SHALLOW:
            i = SHALLOW.index(f)
            shallow_strips(ref, e_ref, o_ref, 4 * T + i, shallow, T * i)
    blank = jnp.zeros((T, 4, NZ), F32)
    e_ref[3 * T : 4 * T, 4:8, :] = blank
    o_ref[3 * T : 4 * T, 4:8, :] = blank
    copies[7].wait()


def beside_y(got, f, rows):
    odd = parity()[1] == 1
    slot, k = f // 2, 4 * (f % 2)
    a, b = (strip[rows(T * slot), k : k + 4, :] for strip in got)
    return jnp.where(odd, a, b), jnp.where(odd, b, a)


def shallow_beside_y(got, i):
    odd = parity()[1] == 1
    a, b = (strip[4 * T + i] for strip in got)
    return jnp.where(odd, a, b), jnp.where(odd, b, a)


def pack_x(*refs):
    fields, shallow, got, (e_ref, o_ref) = refs[:7], refs[7], refs[8:10], refs[10:]
    odd_x = parity()[0]
    for f, ref in enumerate(fields):
        width = WIDTHS[f]
        for low, out in ((odd_x, e_ref), (1 - odd_x, o_ref)):
            first = (1 - low) * (T - width)
            for i in range(width):
                x = first + i
                row = OFFSETS[f] + G * i
                below, above = beside_y(got, f, lambda start: start + x)
                out[row : row + 4, :] = below
                out[row + 4 : row + 20, :] = ref[x]
                out[row + 20 : row + 24, :] = above
    for i in range(len(SHALLOW)):
        row = SHALLOW_ROW + E * i
        below, above = shallow_beside_y(got, i)
        for out in (e_ref, o_ref):
            out[row : row + 8, :] = below
            out[row + 8 : row + 24, :] = shallow[T * i : T * i + T, :]
            out[row + 24 : row + 32, :] = above


def count_planes(wavelet, sx, sy, bits, rx, ry, src_ref, rec_ref, scale_ref):
    x0 = lax.axis_index("tx") * T - T
    y0 = lax.axis_index("ty") * T - H
    for t in range(STEPS):
        scale_ref[t : t + 1, :] = jnp.full((1, NZ), wavelet[t], F32)

    def rows(values):
        grid = lax.broadcasted_iota(jnp.int32, (E, values.shape[1]), 0) + y0
        return jnp.where(grid == values, 1.0, 0.0).astype(F32)

    dims = (((1,), (1,)), ((), ()))
    sign = (2 * bits[...] - 1).astype(F32)
    for values, ys, depth, weight, out in (
        (sx[...], sy[...], SRC_DEPTH, sign, src_ref),
        (rx[...], ry[...], REC_DEPTH, None, rec_ref),
    ):
        left = rows(ys)
        if weight is not None:
            left = left * weight
        grid = lax.broadcasted_iota(jnp.int32, (NZ, values.shape[1]), 0)
        here = grid % SH == depth
        for piece in range(3):
            hit = here & (grid // SH + (x0 + T * piece) == values)
            right = jnp.where(hit, 1.0, 0.0).astype(F32)
            out[piece] = lax.dot_general(left, right, dims, preferred_element_type=F32)


def laplace(ref, x, n, ys, ny):
    rows = pl.ds(x, n)
    lane = lanes((1, 1, NZ))
    center = ref[rows, pl.ds(ys, ny), :]
    total = ref[pl.ds(x + 1, n), pl.ds(ys, ny), :] + ref[pl.ds(x - 1, n), pl.ds(ys, ny), :]
    total = total + ref[rows, pl.ds(ys + 1, ny), :] + ref[rows, pl.ds(ys - 1, ny), :]
    down = jnp.where(lane == NZ - 1, 0.0, turn(center, -1))
    up = jnp.where(lane == 0, 0.0, turn(center, 1))
    return center, total + down + up - 6.0 * center


def shallow_laplace(ref):
    rows = pl.ds(PAD, E)
    lane = lanes((3, E, NZ))
    center = ref[:, rows, :]
    total = ref[:, pl.ds(PAD + 1, E), :] + ref[:, pl.ds(PAD - 1, E), :]
    total = total + jnp.where(lane % SH == SH - 1, 0.0, turn(center, -1))
    total = total + jnp.where(lane % SH == 0, 0.0, turn(center, 1))
    left = turn(center, SH)
    right = turn(center, -SH)
    none = jnp.zeros((1, E, NZ), F32)
    left = jnp.where(lane < SH, jnp.concatenate([none, left[0:2]], 0), left)
    right = jnp.where(lane >= NZ - SH, jnp.concatenate([right[1:3], none], 0), right)
    return center, total + left + right - 6.0 * center


def loop(start, blocks, n, body):
    def step(i, carry):
        body(XO + start + i * n)
        return carry

    lax.fori_loop(0, blocks, step, 0)


ALL_Y = pl.ds(PAD, G)
OWN_Y = pl.ds(PAD + D, T)
OWN_X = pl.ds(XO + D, T)
PLAN = ((0, 4, 6), (2, 5, 4), (3, 3, 6), (4, 4, 4))
WIDE = (G + 2 * XO, G + 2 * PAD, NZ)
FLAT = (G + 2 * XO, G, NZ)
LOW = (3, E + 2 * PAD, NZ)


def clear_ends(ref):
    blank = jnp.zeros((3, PAD, NZ), F32)
    ref[:, 0:PAD, :] = blank
    ref[:, PAD + E : PAD + E + PAD, :] = blank


def assemble(f, ref, ext, got, xe, xo):
    odd = parity()[0] == 1
    ext[OWN_X, OWN_Y, :] = ref[...]
    below, above = beside_y(got, f, lambda start: slice(start, start + T))
    ext[OWN_X, PAD : PAD + 4, :] = below
    ext[OWN_X, PAD + 20 : PAD + 24, :] = above
    width = WIDTHS[f]
    for i in range(width):
        rows = pl.ds(OFFSETS[f] + G * i, G)
        got_e = xe[rows, :]
        got_o = xo[rows, :]
        ext[XO + D - width + i, ALL_Y, :] = jnp.where(odd, got_e, got_o)
        ext[XO + D + T + i, ALL_Y, :] = jnp.where(odd, got_o, got_e)


def assemble_shallow(i, mine, ext, got, xe, xo):
    odd = parity()[0] == 1
    rows = pl.ds(SHALLOW_ROW + E * i, E)
    got_e = xe[rows, :]
    got_o = xo[rows, :]
    ext[0, PAD : PAD + E, :] = jnp.where(odd, got_e, got_o)
    ext[2, PAD : PAD + E, :] = jnp.where(odd, got_o, got_e)
    ext[1, PAD + H : PAD + H + T, :] = mine
    below, above = shallow_beside_y(got, i)
    ext[1, PAD : PAD + H, :] = below
    ext[1, PAD + H + T : PAD + E, :] = above


def background(x, n, scale, now, old, C, SF, t):
    rows = pl.ds(x, n)
    center, lap = laplace(now, x, n, PAD, G)
    accel = C[rows, ALL_Y, :] * lap + scale * SF[rows]
    if t < STEPS - 1:
        old[rows, ALL_Y, :] = 2.0 * center - old[rows, ALL_Y, :] + accel
    return accel


def place_sources(src, SF):
    short = lanes((G, NZ))
    for x in range(1, G - 1):
        piece, at = (x - D + T) // T, SH * ((x - D) % T)
        SF[XO + x] = jnp.where(short == SRC_DEPTH, turn(src[piece, 4:28, :], -at), 0.0)


def free(scales, *refs):
    fields, shallow, got, refs = refs[:7], refs[7], refs[8:10], refs[10:]
    xe, xo, src, SA, CS, BS0, BS1, first, second, IM = refs[:10]
    U0, U1, C, M0, M1, Q0, Q1, SF, A, US = refs[10:]
    rows = pl.ds(PAD, E)

    with jax.named_scope("assemble"):
        for f, ext in ((0, U0), (2, C), (3, M0), (4, U1), (6, M1)):
            assemble(f, fields[f], ext, got, xe, xo)
        for ext in (US.at[0], US.at[1], BS0, BS1):
            clear_ends(ext)
        for i, ext in enumerate((US.at[0], BS1, CS, US.at[1], BS0)):
            assemble_shallow(i, shallow[T * i : T * i + T, :], ext, got, xe, xo)
        place_sources(src, SF)

    with jax.named_scope("shallow"):
        for t in range(STEPS):
            now, old = US.at[t % 2], US.at[1 - t % 2]
            center, lap = shallow_laplace(now)
            accel = CS[:, rows, :] * lap + scales[t : t + 1, :][None] * src[...]
            SA[t] = accel
            if t < STEPS - 1:
                old[:, rows, :] = 2.0 * center - old[:, rows, :] + accel

    waves = (U1, U0)
    for t in range(STEPS):
        with jax.named_scope("forward"):
            old, now = waves
            scale = scales[t : t + 1, :][None]
            start, blocks, n = PLAN[t]

            def forward(x):
                A[t, pl.ds(x, n)] = background(x, n, scale, now, old, C, SF, t)

            loop(start, blocks, n, forward)
            waves = (now, old)

    def scaled(x):
        rows = pl.ds(x, 6)
        Q0[rows, ALL_Y, :] = C[rows, ALL_Y, :] * M0[rows, ALL_Y, :]

    loop(0, 4, 6, scaled)
    upcoming, latest, q_now, q_new = M0, M1, Q0, Q1
    for t in range(STEPS, 1, -1):
        with jax.named_scope("adjoint"):
            start, blocks, n = PLAN[STEPS - t]

            def back(x):
                rows = pl.ds(x, n)
                _, lap = laplace(q_now, x, n, PAD, G)
                current = 2.0 * upcoming[rows, ALL_Y, :] - latest[rows, ALL_Y, :] + lap
                latest[rows, ALL_Y, :] = current
                q_new[rows, ALL_Y, :] = C[rows, ALL_Y, :] * current

            loop(start, blocks, n, back)
            upcoming, latest = latest, upcoming
            q_now, q_new = q_new, q_now

            def gather(x):
                rows = pl.ds(x, 4)
                mine = pl.ds(x - XO - D, 4)
                product = A[t - 1, rows, D : D + T, :] * upcoming[rows, OWN_Y, :]
                IM[mine] = -product if t == STEPS else IM[mine] - product

            loop(D, 4, 4, gather)

    def finish(x):
        rows = pl.ds(x, 4)
        mine = pl.ds(x - XO - D, 4)
        _, lap = laplace(q_now, x, 4, PAD + D, T)
        ahead = upcoming[rows, OWN_Y, :]
        current = 2.0 * ahead - latest[rows, OWN_Y, :] + lap
        first[mine] = current
        second[mine] = ahead
        IM[mine] = IM[mine] - A[0, rows, D : D + T, :] * current

    loop(D, 4, 4, finish)


def meet(SA, CS, BS0, BS1, IM0, windows, rec, image, sent, BS, PS, QS, IM):
    rows = pl.ds(PAD, E)
    with jax.named_scope("turn"):
        planes = jnp.concatenate([windows[pl.ds(s, SH, stride=8), :] for s in range(8)], 0)
        turned = jnp.concatenate([planes, jnp.zeros((64, NZ), F32)], 0).T
        parts = [turned[32 * g : 32 * g + 32, :] for g in range(4)]
        flat = lanes((E, NZ))
        PS[0] = turn(parts[0], 64)
        PS[1] = jnp.where(flat < 64, parts[1], turn(parts[2], 64))
        PS[2] = parts[3]

    with jax.named_scope("shallow"):
        for i in range(STEPS):
            clear_ends(BS.at[i])
        for i in range(2):
            clear_ends(QS.at[i])
        olds = (BS0, BS1, BS.at[0], BS.at[1], BS.at[2], BS.at[3])
        for t in range(STEPS):
            center, lap = shallow_laplace(olds[t + 1])
            olds[t + 2][:, rows, :] = (
                2.0 * center - olds[t][:, rows, :] + CS[:, rows, :] * lap - PS[...] * SA[t]
            )
        own = pl.ds(H, T)
        now = rec[...] * BS[3, :, rows, :]
        older = None
        delta = -SA[3, 1, own, :] * now[1, H : H + T, :]
        for t in (3, 2, 1):
            QS[t % 2, :, rows, :] = CS[:, rows, :] * now
            _, lap = shallow_laplace(QS.at[t % 2])
            new = 2.0 * now + lap + rec[...] * BS[t - 1, :, rows, :]
            if older is not None:
                new = new - older
            now, older = new, now
            delta = delta - SA[t - 1, 1, own, :] * now[1, H : H + T, :]
        sent[0] = now[1, H : H + T, :]
        sent[1] = older[1, H : H + T, :]

    with jax.named_scope("image"):
        here = lanes((T, NZ)) < SH
        for x in range(T):
            IM[x] = IM0[x] + jnp.where(here, turn(delta, -SH * x), 0.0)
        for half in range(2):
            turned = IM[8 * half : 8 * half + 8].reshape(128, NZ).T
            for shot in range(2):
                image[pl.ds(256 * shot + half, 128, stride=2), :] = turned


def born(scales, *refs):
    fields, got, refs = refs[:7], refs[7:9], refs[9:]
    xe, xo, src, windows, first0, second0, sent, last, before, first, second, U0, U1, C, PT, B, SF = refs
    for f, ext in ((0, U0), (1, B.at[1]), (2, C), (4, U1), (5, B.at[0])):
        assemble(f, fields[f], ext, got, xe, xo)
    place_sources(src, SF)
    for s in range(8):
        turned = windows[pl.ds(s, NZ, stride=8), :].T
        for g in range(4):
            PT[8 * g + s] = turned[32 * g : 32 * g + 32, :]
    waves = (U1, U0)
    for t in range(STEPS):
        old, now = waves
        scale = scales[t : t + 1, :][None]
        start, blocks, n = PLAN[t]

        def step(x):
            rows = pl.ds(x, n)
            accel = background(x, n, scale, now, old, C, SF, t)
            center, lap = laplace(B.at[t + 1], x, n, PAD, G)
            B[t + 2, rows, ALL_Y, :] = (
                2.0 * center - B[t, rows, ALL_Y, :] + C[rows, ALL_Y, :] * lap
                - PT[pl.ds(x - XO + 4, n), 4:28, :] * accel
            )

        loop(start, blocks, n, step)
        waves = (now, old)
    last[...] = B[STEPS + 1, OWN_X, OWN_Y, :]
    before[...] = B[STEPS, OWN_X, OWN_Y, :]
    here = lanes((T, NZ)) < SH
    for x in range(T):
        first[x] = first0[x] + jnp.where(here, turn(sent[0], -SH * x), 0.0)
        second[x] = second0[x] + jnp.where(here, turn(sent[1], -SH * x), 0.0)


def arrange(arrived, out):
    first = lax.axis_index("shot") * 16
    lane = lanes((8, NZ))
    for half in range(2):
        groups = []
        for j in range(8):
            groups.append(
                arrived[pl.ds(first + 2 * j + half, 8, stride=32), :]
                + arrived[pl.ds(first + 256 + 2 * j + half, 8, stride=32), :]
            )
        for k in range(8):
            line = jnp.zeros((8, NZ), F32)
            for j in range(8):
                line = jnp.where((lane >= 16 * j) & (lane < 16 * j + 16), turn(groups[j], 16 * j - 16 * k), line)
            out[pl.ds(8 * half + k, 8, stride=16), :] = line


def swap(cells, axis, odd):
    count = lax.axis_size(axis)
    pairs = [(i, ((i - odd) ^ 1) + odd) for i in range(odd, count - odd)]
    return lax.ppermute(cells, axis, pairs)


def per_device(
    perturbation, courant_sq, background_prev, background_now, born_prev, born_now,
    adjoint_next, adjoint_after, encode_bits, wavelet, source_x, source_y, receiver_x, receiver_y,
):
    shape = lambda *dims: jax.ShapeDtypeStruct(dims, F32)
    tile = (T, T, NZ)
    fields = [
        a.reshape(tile)
        for a in (background_now, born_now, courant_sq, adjoint_next, background_prev, born_prev, adjoint_after)
    ]

    strip = shape(*STRIP_Y)
    send_e, send_o, shallow, *fields, plane = call(
        pack_fields,
        (strip, strip, shape(5 * T, NZ)) + (shape(*tile),) * 7 + (shape(128, 256),),
        [HBM] * 8,
        [pltpu.SemaphoreType.DMA((8,))],
    )(*[pltpu.with_memory_space_constraint(a, pltpu.HBM) for a in (*fields, perturbation.reshape(128, 256))])
    got = (swap(send_e, "ty", 0), swap(send_o, "ty", 1))
    blocks = call(pack_windows, shape(128, 8, 128), [VMEM])(plane)
    windows = lax.all_to_all(blocks, ("tx", "ty"), split_axis=0, concat_axis=0, tiled=True).reshape(1024, NZ)
    strip = shape(*STRIP_X)
    send_e, send_o = call(pack_x, (strip, strip), [VMEM] * 10, cost=BUSY)(*fields, shallow, *got)
    across = (swap(send_e, "tx", 0), swap(send_o, "tx", 1))
    pieces = shape(3, E, NZ)
    src, rec, scales = call(count_planes, (pieces, pieces, shape(8, NZ)), [SMEM] + [VMEM] * 5)(
        wavelet, source_x[None], source_y[None], encode_bits, receiver_x[None], receiver_y[None]
    )

    one = lambda *dims: pltpu.VMEM(dims, F32)
    cells = shape(*tile)
    low = shape(*LOW)
    SA, CS, BS0, BS1, first, second, IM = call(
        free,
        (shape(STEPS, 3, E, NZ), low, low, low, cells, cells, cells),
        [VMEM] * 14,
        [one(*WIDE)] * 7 + [one(*FLAT), one(STEPS, *FLAT), one(2, *LOW)],
    )(scales, *fields, shallow, *got, *across, src)
    image, sent = call(
        meet,
        (shape(512, NZ), shape(2, T, NZ)),
        [VMEM] * 7,
        [one(4, *LOW), one(3, E, NZ), one(2, *LOW), one(*tile)],
    )(SA, CS, BS0, BS1, IM, windows, rec)
    last, before, first, second = call(
        born,
        (cells, cells, cells, cells),
        [VMEM] * 17,
        [one(*WIDE)] * 3 + [one(E, E, NZ), one(STEPS + 2, *WIDE), one(*FLAT)],
    )(scales, *fields, *got, *across, src, windows, first, second, sent)

    arrived = lax.all_to_all(
        image.reshape(256, 2, NZ), ("shot", "tx", "ty"), split_axis=0, concat_axis=0, tiled=True
    )
    hessian = call(arrange, shape(128, NZ), [VMEM])(arrived.reshape(512, NZ))
    return (hessian[None], first[None], second[None], last[None], before[None])


def solution(mesh):
    field = P("shot", "tx", "ty", None)
    placed = (
        P(("tx", "ty"), None, None),
        P("tx", "ty", None),
        field, field, field, field, field, field,
        P("shot", None),
        P(), P(), P(), P(), P(),
    )
    return jax.shard_map(
        per_device,
        mesh=mesh,
        in_specs=placed,
        out_specs=(P(("tx", "ty"), None, "shot"), field, field, field, field),
        check_vma=False,
    )
```

```python
import jax
import jax.numpy as jnp
from jax import lax
from jax.experimental import pallas as pl
from jax.experimental.pallas import tpu as pltpu
from jax.sharding import PartitionSpec as P

STEPS = 4
SRC_DEPTH = 4
REC_DEPTH = 2
NZ = 128
T = 16
D = 4
G = T + 2 * D
H = 8
E = T + 2 * H
PAD = 8
XO = 1
SH = 8
WIDTHS = (4, 4, 4, 4, 3, 3, 3)
OFFSETS = tuple(sum(WIDTHS[:i]) * G for i in range(len(WIDTHS)))
SHALLOW = (0, 1, 2, 4, 5)
SHALLOW_ROW = sum(WIDTHS) * G
STRIP_Y = (4 * T + 5, 8, NZ)
STRIP_X = (SHALLOW_ROW + len(SHALLOW) * E, NZ)
F32 = jnp.float32
VMEM = pl.BlockSpec(memory_space=pltpu.VMEM)
SMEM = pl.BlockSpec(memory_space=pltpu.SMEM)
HBM = pl.BlockSpec(memory_space=pltpu.HBM)


BUSY = pl.CostEstimate(flops=10**15, bytes_accessed=10**9, transcendentals=0)


def call(body, outs, specs, scratch=(), mib=32, cost=None):
    return pl.pallas_call(
        body,
        out_shape=outs,
        in_specs=specs,
        out_specs=jax.tree.map(lambda _: VMEM, outs),
        scratch_shapes=list(scratch),
        compiler_params=pltpu.CompilerParams(vmem_limit_bytes=mib and mib * 1024 * 1024),
        cost_estimate=cost,
    )


def lanes(shape):
    return lax.broadcasted_iota(jnp.int32, shape, len(shape) - 1)


def turn(piece, amount):
    amount = amount % NZ
    return pltpu.roll(piece, amount, len(piece.shape) - 1) if amount else piece


def pack_windows(plane_ref, out_ref, left, right):
    lane = lanes((8, NZ))
    sub = lax.broadcasted_iota(jnp.int32, (8, NZ), 0)
    zero = jnp.zeros((8, NZ), F32)
    for half, side in enumerate((left, right)):
        side[0:8, :] = zero
        side[136:144, :] = zero
        side[8:136, :] = plane_ref[:, NZ * half : NZ * half + NZ]

    def put(block, row, start, at, where=None):
        for half, side in enumerate((left, right)):
            lo = max(start, NZ * half)
            hi = min(start + 32, NZ * half + NZ)
            if lo >= hi:
                continue
            here = (lane >= at + lo - start) & (lane < at + hi - start)
            if where is not None:
                here = here & where
            block = jnp.where(here, turn(side[8 + row : 16 + row, :], at - start), block)
        return block

    for chip in range(4):
        for pair in range(8):
            rest = zero
            for odd in range(2):
                start = 16 * (2 * pair + odd) - 8
                main = zero
                for g in range(6):
                    row = 32 * chip - 8 + 8 * g
                    if row < 0 or row >= 128:
                        continue
                    if g < 4:
                        main = put(main, row, start, 32 * g)
                    else:
                        mine = (sub >= 4) if odd else (sub < 4)
                        rest = put(rest, row - 4 * odd, start, 32 * (g - 4), mine)
                        rest = put(rest, row + 4 - 4 * odd, start, 64 + 32 * (g - 4), mine)
                base = 24 * (8 * chip + pair)
                out_ref[base + 16 * odd : base + 16 * odd + 8, :] = main
            out_ref[base + 8 : base + 16, :] = rest


def split_windows(arrived, mine, other):
    core = parity()[0] == 1
    odd = parity()[1]
    lane = lanes((8, 128))
    for k in range(64):
        main = arrived[pl.ds(12 * k + 4 * odd, 8), :]
        rest = arrived[pl.ds(12 * k + 8 - 8 * odd, 4), :]
        rest = jnp.concatenate([turn(rest, 64), rest], 0)
        upper = jnp.where(lane < 64, turn(main, 64), rest)
        mine[8 * k : 8 * k + 8, :] = jnp.where(core, upper, main)
        other[8 * k : 8 * k + 8, :] = jnp.where(core, main, upper)


def parity():
    return lax.rem(lax.axis_index("tx"), 2), lax.rem(lax.axis_index("ty"), 2)


def strips(ref, e_ref, o_ref, row, k):
    odd = parity()[1] == 1
    low = ref[:, 0:4, :]
    high = ref[:, 12:16, :]
    e_ref[row : row + T, k : k + 4, :] = jnp.where(odd, low, high)
    o_ref[row : row + T, k : k + 4, :] = jnp.where(odd, high, low)


def shallow_strips(ref, e_ref, o_ref, row, shallow, at):
    odd = parity()[1] == 1
    lane = lanes((T, NZ))
    packed = ref[0]
    for x in range(1, T):
        packed = jnp.where(lane >= SH * x, turn(ref[x], SH * x), packed)
    shallow[at : at + T, :] = packed
    e_ref[row] = jnp.where(odd, packed[0:8], packed[8:16])
    o_ref[row] = jnp.where(odd, packed[8:16], packed[0:8])


def pack_fields(*refs):
    sources, (e_ref, o_ref, shallow), targets, sems = refs[:8], refs[8:11], refs[11:19], refs[19]
    copies = [pltpu.make_async_copy(a, b, sems.at[i]) for i, (a, b) in enumerate(zip(sources, targets))]
    for copy in copies:
        copy.start()
    for f, ref in enumerate(targets[:7]):
        copies[f].wait()
        strips(ref, e_ref, o_ref, T * (f // 2), 4 * (f % 2))
        if f in SHALLOW:
            i = SHALLOW.index(f)
            shallow_strips(ref, e_ref, o_ref, 4 * T + i, shallow, T * i)
    blank = jnp.zeros((T, 4, NZ), F32)
    e_ref[3 * T : 4 * T, 4:8, :] = blank
    o_ref[3 * T : 4 * T, 4:8, :] = blank
    copies[7].wait()


def beside_y(got, f, rows):
    odd = parity()[1] == 1
    slot, k = f // 2, 4 * (f % 2)
    a, b = (strip[rows(T * slot), k : k + 4, :] for strip in got)
    return jnp.where(odd, a, b), jnp.where(odd, b, a)


def shallow_beside_y(got, i):
    odd = parity()[1] == 1
    a, b = (strip[4 * T + i] for strip in got)
    return jnp.where(odd, a, b), jnp.where(odd, b, a)


def pack_x(*refs):
    fields, shallow, got, (e_ref, o_ref) = refs[:7], refs[7], refs[8:10], refs[10:]
    odd_x = parity()[0]
    for f, ref in enumerate(fields):
        width = WIDTHS[f]
        for low, out in ((odd_x, e_ref), (1 - odd_x, o_ref)):
            first = (1 - low) * (T - width)
            for i in range(width):
                x = first + i
                row = OFFSETS[f] + G * i
                below, above = beside_y(got, f, lambda start: start + x)
                out[row : row + 4, :] = below
                out[row + 4 : row + 20, :] = ref[x]
                out[row + 20 : row + 24, :] = above
    for i in range(len(SHALLOW)):
        row = SHALLOW_ROW + E * i
        below, above = shallow_beside_y(got, i)
        for out in (e_ref, o_ref):
            out[row : row + 8, :] = below
            out[row + 8 : row + 24, :] = shallow[T * i : T * i + T, :]
            out[row + 24 : row + 32, :] = above


def count_planes(wavelet, sx, sy, bits, rx, ry, src_ref, rec_ref, scale_ref):
    x0 = lax.axis_index("tx") * T - T
    y0 = lax.axis_index("ty") * T - H
    for t in range(STEPS):
        scale_ref[t : t + 1, :] = jnp.full((1, NZ), wavelet[t], F32)

    def rows(values):
        grid = lax.broadcasted_iota(jnp.int32, (E, values.shape[1]), 0) + y0
        return jnp.where(grid == values, 1.0, 0.0).astype(F32)

    dims = (((1,), (1,)), ((), ()))
    sign = (2 * bits[...] - 1).astype(F32)
    for values, ys, depth, weight, out in (
        (sx[...], sy[...], SRC_DEPTH, sign, src_ref),
        (rx[...], ry[...], REC_DEPTH, None, rec_ref),
    ):
        left = rows(ys)
        if weight is not None:
            left = left * weight
        grid = lax.broadcasted_iota(jnp.int32, (NZ, values.shape[1]), 0)
        here = grid % SH == depth
        for piece in range(3):
            hit = here & (grid // SH + (x0 + T * piece) == values)
            right = jnp.where(hit, 1.0, 0.0).astype(F32)
            out[piece] = lax.dot_general(left, right, dims, preferred_element_type=F32)


def laplace(ref, x, n, ys, ny):
    rows = pl.ds(x, n)
    lane = lanes((1, 1, NZ))
    center = ref[rows, pl.ds(ys, ny), :]
    total = ref[pl.ds(x + 1, n), pl.ds(ys, ny), :] + ref[pl.ds(x - 1, n), pl.ds(ys, ny), :]
    total = total + ref[rows, pl.ds(ys + 1, ny), :] + ref[rows, pl.ds(ys - 1, ny), :]
    down = jnp.where(lane == NZ - 1, 0.0, turn(center, -1))
    up = jnp.where(lane == 0, 0.0, turn(center, 1))
    return center, total + down + up - 6.0 * center


def shallow_laplace(ref):
    rows = pl.ds(PAD, E)
    lane = lanes((3, E, NZ))
    center = ref[:, rows, :]
    total = ref[:, pl.ds(PAD + 1, E), :] + ref[:, pl.ds(PAD - 1, E), :]
    total = total + jnp.where(lane % SH == SH - 1, 0.0, turn(center, -1))
    total = total + jnp.where(lane % SH == 0, 0.0, turn(center, 1))
    left = turn(center, SH)
    right = turn(center, -SH)
    none = jnp.zeros((1, E, NZ), F32)
    left = jnp.where(lane < SH, jnp.concatenate([none, left[0:2]], 0), left)
    right = jnp.where(lane >= NZ - SH, jnp.concatenate([right[1:3], none], 0), right)
    return center, total + left + right - 6.0 * center


def loop(start, blocks, n, body):
    def step(i, carry):
        body(XO + start + i * n)
        return carry

    lax.fori_loop(0, blocks, step, 0)


ALL_Y = pl.ds(PAD, G)
OWN_Y = pl.ds(PAD + D, T)
OWN_X = pl.ds(XO + D, T)
PLAN = ((0, 4, 6), (2, 5, 4), (3, 3, 6), (4, 4, 4))
WIDE = (G + 2 * XO, G + 2 * PAD, NZ)
FLAT = (G + 2 * XO, G, NZ)
LOW = (3, E + 2 * PAD, NZ)


def clear_ends(ref):
    blank = jnp.zeros((3, PAD, NZ), F32)
    ref[:, 0:PAD, :] = blank
    ref[:, PAD + E : PAD + E + PAD, :] = blank


def assemble(f, ref, ext, got, xe, xo):
    odd = parity()[0] == 1
    ext[OWN_X, OWN_Y, :] = ref[...]
    below, above = beside_y(got, f, lambda start: slice(start, start + T))
    ext[OWN_X, PAD : PAD + 4, :] = below
    ext[OWN_X, PAD + 20 : PAD + 24, :] = above
    width = WIDTHS[f]
    for i in range(width):
        rows = pl.ds(OFFSETS[f] + G * i, G)
        got_e = xe[rows, :]
        got_o = xo[rows, :]
        ext[XO + D - width + i, ALL_Y, :] = jnp.where(odd, got_e, got_o)
        ext[XO + D + T + i, ALL_Y, :] = jnp.where(odd, got_o, got_e)


def assemble_shallow(i, mine, ext, got, xe, xo):
    odd = parity()[0] == 1
    rows = pl.ds(SHALLOW_ROW + E * i, E)
    got_e = xe[rows, :]
    got_o = xo[rows, :]
    ext[0, PAD : PAD + E, :] = jnp.where(odd, got_e, got_o)
    ext[2, PAD : PAD + E, :] = jnp.where(odd, got_o, got_e)
    ext[1, PAD + H : PAD + H + T, :] = mine
    below, above = shallow_beside_y(got, i)
    ext[1, PAD : PAD + H, :] = below
    ext[1, PAD + H + T : PAD + E, :] = above


def background(x, n, scale, now, old, C, SF, t):
    rows = pl.ds(x, n)
    center, lap = laplace(now, x, n, PAD, G)
    accel = C[rows, ALL_Y, :] * lap + scale * SF[rows]
    if t < STEPS - 1:
        old[rows, ALL_Y, :] = 2.0 * center - old[rows, ALL_Y, :] + accel
    return accel


def place_sources(src, SF):
    short = lanes((G, NZ))
    for x in range(1, G - 1):
        piece, at = (x - D + T) // T, SH * ((x - D) % T)
        SF[XO + x] = jnp.where(short == SRC_DEPTH, turn(src[piece, 4:28, :], -at), 0.0)


def free(scales, *refs):
    fields, shallow, got, refs = refs[:7], refs[7], refs[8:10], refs[10:]
    xe, xo, src, SA, CS, BS0, BS1, first, second, IM = refs[:10]
    U0, U1, C, M0, M1, Q0, Q1, SF, A, US = refs[10:]
    rows = pl.ds(PAD, E)

    with jax.named_scope("assemble"):
        for f, ext in ((0, U0), (2, C), (3, M0), (4, U1), (6, M1)):
            assemble(f, fields[f], ext, got, xe, xo)
        for ext in (US.at[0], US.at[1], BS0, BS1):
            clear_ends(ext)
        for i, ext in enumerate((US.at[0], BS1, CS, US.at[1], BS0)):
            assemble_shallow(i, shallow[T * i : T * i + T, :], ext, got, xe, xo)
        place_sources(src, SF)

    with jax.named_scope("shallow"):
        for t in range(STEPS):
            now, old = US.at[t % 2], US.at[1 - t % 2]
            center, lap = shallow_laplace(now)
            accel = CS[:, rows, :] * lap + scales[t : t + 1, :][None] * src[...]
            SA[t] = accel
            if t < STEPS - 1:
                old[:, rows, :] = 2.0 * center - old[:, rows, :] + accel

    waves = (U1, U0)
    for t in range(STEPS):
        with jax.named_scope("forward"):
            old, now = waves
            scale = scales[t : t + 1, :][None]
            start, blocks, n = PLAN[t]

            def forward(x):
                A[t, pl.ds(x, n)] = background(x, n, scale, now, old, C, SF, t)

            loop(start, blocks, n, forward)
            waves = (now, old)

    def scaled(x):
        rows = pl.ds(x, 6)
        Q0[rows, ALL_Y, :] = C[rows, ALL_Y, :] * M0[rows, ALL_Y, :]

    loop(0, 4, 6, scaled)
    upcoming, latest, q_now, q_new = M0, M1, Q0, Q1
    for t in range(STEPS, 1, -1):
        with jax.named_scope("adjoint"):
            start, blocks, n = PLAN[STEPS - t]

            def back(x):
                rows = pl.ds(x, n)
                _, lap = laplace(q_now, x, n, PAD, G)
                current = 2.0 * upcoming[rows, ALL_Y, :] - latest[rows, ALL_Y, :] + lap
                latest[rows, ALL_Y, :] = current
                q_new[rows, ALL_Y, :] = C[rows, ALL_Y, :] * current

            loop(start, blocks, n, back)
            upcoming, latest = latest, upcoming
            q_now, q_new = q_new, q_now

            def gather(x):
                rows = pl.ds(x, 4)
                mine = pl.ds(x - XO - D, 4)
                product = A[t - 1, rows, D : D + T, :] * upcoming[rows, OWN_Y, :]
                IM[mine] = -product if t == STEPS else IM[mine] - product

            loop(D, 4, 4, gather)

    def finish(x):
        rows = pl.ds(x, 4)
        mine = pl.ds(x - XO - D, 4)
        _, lap = laplace(q_now, x, 4, PAD + D, T)
        ahead = upcoming[rows, OWN_Y, :]
        current = 2.0 * ahead - latest[rows, OWN_Y, :] + lap
        first[mine] = current
        second[mine] = ahead
        IM[mine] = IM[mine] - A[0, rows, D : D + T, :] * current

    loop(D, 4, 4, finish)


def meet(SA, CS, BS0, BS1, IM0, mine, got, rec, image, sent, BS, PS, QS, IM):
    rows = pl.ds(PAD, E)
    with jax.named_scope("turn"):
        core = parity()[0] == 1
        planes = [jnp.where(core, got[pl.ds(s, SH, stride=8), :], mine[pl.ds(s, SH, stride=8), :]) for s in range(8)]
        planes = jnp.concatenate(planes, 0)
        turned = jnp.concatenate([planes, jnp.zeros((64, NZ), F32)], 0).T
        parts = [turned[32 * g : 32 * g + 32, :] for g in range(4)]
        flat = lanes((E, NZ))
        PS[0] = turn(parts[0], 64)
        PS[1] = jnp.where(flat < 64, parts[1], turn(parts[2], 64))
        PS[2] = parts[3]

    with jax.named_scope("shallow"):
        for i in range(STEPS):
            clear_ends(BS.at[i])
        for i in range(2):
            clear_ends(QS.at[i])
        olds = (BS0, BS1, BS.at[0], BS.at[1], BS.at[2], BS.at[3])
        for t in range(STEPS):
            center, lap = shallow_laplace(olds[t + 1])
            olds[t + 2][:, rows, :] = (
                2.0 * center - olds[t][:, rows, :] + CS[:, rows, :] * lap - PS[...] * SA[t]
            )
        own = pl.ds(H, T)
        now = rec[...] * BS[3, :, rows, :]
        older = None
        delta = -SA[3, 1, own, :] * now[1, H : H + T, :]
        for t in (3, 2, 1):
            QS[t % 2, :, rows, :] = CS[:, rows, :] * now
            _, lap = shallow_laplace(QS.at[t % 2])
            new = 2.0 * now + lap + rec[...] * BS[t - 1, :, rows, :]
            if older is not None:
                new = new - older
            now, older = new, now
            delta = delta - SA[t - 1, 1, own, :] * now[1, H : H + T, :]
        sent[0] = now[1, H : H + T, :]
        sent[1] = older[1, H : H + T, :]

    with jax.named_scope("image"):
        here = lanes((T, NZ)) < SH
        for x in range(T):
            IM[x] = IM0[x] + jnp.where(here, turn(delta, -SH * x), 0.0)
        for half in range(2):
            turned = IM[8 * half : 8 * half + 8].reshape(128, NZ).T
            for shot in range(2):
                image[pl.ds(256 * shot + half, 128, stride=2), :] = turned


def born(scales, *refs):
    fields, got, refs = refs[:7], refs[7:9], refs[9:]
    xe, xo, src, near, far, first0, second0, sent, last, before, first, second, U0, U1, C, PT, B, SF = refs
    for f, ext in ((0, U0), (1, B.at[1]), (2, C), (4, U1), (5, B.at[0])):
        assemble(f, fields[f], ext, got, xe, xo)
    place_sources(src, SF)
    core = parity()[0] == 1
    for s in range(8):
        planes = []
        for k in range(4):
            rows = pl.ds(128 * k + s, T, stride=8)
            a, b = near[rows, :], far[rows, :]
            planes += [jnp.where(core, b, a), jnp.where(core, a, b)]
        turned = jnp.concatenate(planes, 0).T
        for g in range(4):
            PT[8 * g + s] = turned[32 * g : 32 * g + 32, :]
    waves = (U1, U0)
    for t in range(STEPS):
        old, now = waves
        scale = scales[t : t + 1, :][None]
        start, blocks, n = PLAN[t]

        def step(x):
            rows = pl.ds(x, n)
            accel = background(x, n, scale, now, old, C, SF, t)
            center, lap = laplace(B.at[t + 1], x, n, PAD, G)
            B[t + 2, rows, ALL_Y, :] = (
                2.0 * center - B[t, rows, ALL_Y, :] + C[rows, ALL_Y, :] * lap
                - PT[pl.ds(x - XO + 4, n), 4:28, :] * accel
            )

        loop(start, blocks, n, step)
        waves = (now, old)
    last[...] = B[STEPS + 1, OWN_X, OWN_Y, :]
    before[...] = B[STEPS, OWN_X, OWN_Y, :]
    here = lanes((T, NZ)) < SH
    for x in range(T):
        first[x] = first0[x] + jnp.where(here, turn(sent[0], -SH * x), 0.0)
        second[x] = second0[x] + jnp.where(here, turn(sent[1], -SH * x), 0.0)


def arrange(arrived, out):
    first = lax.axis_index("shot") * 16
    lane = lanes((8, NZ))
    for half in range(2):
        groups = []
        for j in range(8):
            groups.append(
                arrived[pl.ds(first + 2 * j + half, 8, stride=32), :]
                + arrived[pl.ds(first + 256 + 2 * j + half, 8, stride=32), :]
            )
        for k in range(8):
            line = jnp.zeros((8, NZ), F32)
            for j in range(8):
                line = jnp.where((lane >= 16 * j) & (lane < 16 * j + 16), turn(groups[j], 16 * j - 16 * k), line)
            out[pl.ds(8 * half + k, 8, stride=16), :] = line


def swap(cells, axis, odd):
    count = lax.axis_size(axis)
    pairs = [(i, ((i - odd) ^ 1) + odd) for i in range(odd, count - odd)]
    return lax.ppermute(cells, axis, pairs)


def per_device(
    perturbation, courant_sq, background_prev, background_now, born_prev, born_now,
    adjoint_next, adjoint_after, encode_bits, wavelet, source_x, source_y, receiver_x, receiver_y,
):
    shape = lambda *dims: jax.ShapeDtypeStruct(dims, F32)
    tile = (T, T, NZ)
    fields = [
        a.reshape(tile)
        for a in (background_now, born_now, courant_sq, adjoint_next, background_prev, born_prev, adjoint_after)
    ]

    strip = shape(*STRIP_Y)
    send_e, send_o, shallow, *fields, plane = call(
        pack_fields,
        (strip, strip, shape(5 * T, NZ)) + (shape(*tile),) * 7 + (shape(128, 256),),
        [HBM] * 8,
        [pltpu.SemaphoreType.DMA((8,))],
    )(*[pltpu.with_memory_space_constraint(a, pltpu.HBM) for a in (*fields, perturbation.reshape(128, 256))])
    got = (swap(send_e, "ty", 0), swap(send_o, "ty", 1))
    side = pltpu.VMEM((144, NZ), F32)
    blocks = call(pack_windows, shape(768, NZ), [VMEM], [side, side])(plane)
    groups = [[(2 * chip + core) * 16 + ty for chip in range(4) for ty in range(16)] for core in range(2)]
    windows = lax.all_to_all(
        blocks.reshape(192, 4, NZ), ("tx", "ty"), split_axis=0, concat_axis=0, tiled=True, axis_index_groups=groups
    ).reshape(768, NZ)
    pieces = shape(3, E, NZ)
    src, rec, scales = call(count_planes, (pieces, pieces, shape(8, NZ)), [SMEM] + [VMEM] * 5)(
        wavelet, source_x[None], source_y[None], encode_bits, receiver_x[None], receiver_y[None]
    )
    windows, src, rec, scales = lax.optimization_barrier((windows, src, rec, scales))
    near, other = call(split_windows, (shape(512, NZ), shape(512, NZ)), [VMEM])(windows)
    far = swap(other, "tx", 0)
    strip = shape(*STRIP_X)
    send_e, send_o = call(pack_x, (strip, strip), [VMEM] * 10, cost=BUSY)(*fields, shallow, *got)
    across = (swap(send_e, "tx", 0), swap(send_o, "tx", 1))
    one = lambda *dims: pltpu.VMEM(dims, F32)
    cells = shape(*tile)
    low = shape(*LOW)
    SA, CS, BS0, BS1, first, second, IM = call(
        free,
        (shape(STEPS, 3, E, NZ), low, low, low, cells, cells, cells),
        [VMEM] * 14,
        [one(*WIDE)] * 7 + [one(*FLAT), one(STEPS, *FLAT), one(2, *LOW)],
    )(scales, *fields, shallow, *got, *across, src)
    image, sent = call(
        meet,
        (shape(512, NZ), shape(2, T, NZ)),
        [VMEM] * 8,
        [one(4, *LOW), one(3, E, NZ), one(2, *LOW), one(*tile)],
    )(SA, CS, BS0, BS1, IM, near, far, rec)
    last, before, first, second = call(
        born,
        (cells, cells, cells, cells),
        [VMEM] * 18,
        [one(*WIDE)] * 3 + [one(E, E, NZ), one(STEPS + 2, *WIDE), one(*FLAT)],
    )(scales, *fields, *got, *across, src, near, far, first, second, sent)

    arrived = lax.all_to_all(
        image.reshape(256, 2, NZ), ("shot", "tx", "ty"), split_axis=0, concat_axis=0, tiled=True
    )
    hessian = call(arrange, shape(128, NZ), [VMEM])(arrived.reshape(512, NZ))
    return (hessian[None], first[None], second[None], last[None], before[None])


def solution(mesh):
    field = P("shot", "tx", "ty", None)
    placed = (
        P(("tx", "ty"), None, None),
        P("tx", "ty", None),
        field, field, field, field, field, field,
        P("shot", None),
        P(), P(), P(), P(), P(),
    )
    return jax.shard_map(
        per_device,
        mesh=mesh,
        in_specs=placed,
        out_specs=(P(("tx", "ty"), None, "shot"), field, field, field, field),
        check_vma=False,
    )
```

```python
import jax
import jax.numpy as jnp
from jax import lax
from jax.experimental import pallas as pl
from jax.experimental.pallas import tpu as pltpu
from jax.sharding import PartitionSpec as P

STEPS = 4
SRC_DEPTH = 4
REC_DEPTH = 2
NZ = 128
T = 16
D = 4
G = T + 2 * D
H = 8
E = T + 2 * H
PAD = 8
XO = 1
SH = 8
WIDTHS = (4, 4, 4, 4, 3, 3, 3)
OFFSETS = tuple(sum(WIDTHS[:i]) * G for i in range(len(WIDTHS)))
SHALLOW = (0, 1, 2, 4, 5)
SHALLOW_ROW = sum(WIDTHS) * G
STRIP_Y = (4 * T + 5, 8, NZ)
STRIP_X = (SHALLOW_ROW + len(SHALLOW) * E, NZ)
F32 = jnp.float32
VMEM = pl.BlockSpec(memory_space=pltpu.VMEM)
SMEM = pl.BlockSpec(memory_space=pltpu.SMEM)
HBM = pl.BlockSpec(memory_space=pltpu.HBM)


BUSY = pl.CostEstimate(flops=10**15, bytes_accessed=10**9, transcendentals=0)


def call(body, outs, specs, scratch=(), mib=20, cost=None):
    return pl.pallas_call(
        body,
        out_shape=outs,
        in_specs=specs,
        out_specs=jax.tree.map(lambda _: VMEM, outs),
        scratch_shapes=list(scratch),
        compiler_params=pltpu.CompilerParams(vmem_limit_bytes=mib and mib * 1024 * 1024),
        cost_estimate=cost,
    )


def lanes(shape):
    return lax.broadcasted_iota(jnp.int32, shape, len(shape) - 1)


def turn(piece, amount):
    amount = amount % NZ
    return pltpu.roll(piece, amount, len(piece.shape) - 1) if amount else piece


def pack_windows(plane_ref, out_ref, left, right):
    lane = lanes((8, NZ))
    sub = lax.broadcasted_iota(jnp.int32, (8, NZ), 0)
    zero = jnp.zeros((8, NZ), F32)
    for half, side in enumerate((left, right)):
        side[0:8, :] = zero
        side[136:144, :] = zero
        side[8:136, :] = plane_ref[:, NZ * half : NZ * half + NZ]

    def put(block, row, start, at, where=None):
        for half, side in enumerate((left, right)):
            lo = max(start, NZ * half)
            hi = min(start + 32, NZ * half + NZ)
            if lo >= hi:
                continue
            here = (lane >= at + lo - start) & (lane < at + hi - start)
            if where is not None:
                here = here & where
            block = jnp.where(here, turn(side[8 + row : 16 + row, :], at - start), block)
        return block

    for chip in range(4):
        for pair in range(8):
            rest = zero
            for odd in range(2):
                start = 16 * (2 * pair + odd) - 8
                main = zero
                for g in range(6):
                    row = 32 * chip - 8 + 8 * g
                    if row < 0 or row >= 128:
                        continue
                    if g < 4:
                        main = put(main, row, start, 32 * g)
                    else:
                        mine = (sub >= 4) if odd else (sub < 4)
                        rest = put(rest, row - 4 * odd, start, 32 * (g - 4), mine)
                        rest = put(rest, row + 4 - 4 * odd, start, 64 + 32 * (g - 4), mine)
                base = 24 * (8 * chip + pair)
                out_ref[base + 16 * odd : base + 16 * odd + 8, :] = main
            out_ref[base + 8 : base + 16, :] = rest


def split_windows(arrived, mine, other):
    core = parity()[0] == 1
    odd = parity()[1]
    lane = lanes((8, 128))
    for k in range(64):
        main = arrived[pl.ds(12 * k + 4 * odd, 8), :]
        rest = arrived[pl.ds(12 * k + 8 - 8 * odd, 4), :]
        rest = jnp.concatenate([turn(rest, 64), rest], 0)
        upper = jnp.where(lane < 64, turn(main, 64), rest)
        mine[8 * k : 8 * k + 8, :] = jnp.where(core, upper, main)
        other[8 * k : 8 * k + 8, :] = jnp.where(core, main, upper)


def parity():
    return lax.rem(lax.axis_index("tx"), 2), lax.rem(lax.axis_index("ty"), 2)


def strips(ref, e_ref, o_ref, row, k):
    odd = parity()[1] == 1
    low = ref[:, 0:4, :]
    high = ref[:, 12:16, :]
    e_ref[row : row + T, k : k + 4, :] = jnp.where(odd, low, high)
    o_ref[row : row + T, k : k + 4, :] = jnp.where(odd, high, low)


def shallow_strips(ref, e_ref, o_ref, row, shallow, at):
    odd = parity()[1] == 1
    lane = lanes((T, NZ))
    packed = ref[0]
    for x in range(1, T):
        packed = jnp.where(lane >= SH * x, turn(ref[x], SH * x), packed)
    shallow[at : at + T, :] = packed
    e_ref[row] = jnp.where(odd, packed[0:8], packed[8:16])
    o_ref[row] = jnp.where(odd, packed[8:16], packed[0:8])


def pack_fields(*refs):
    sources, (e_ref, o_ref, shallow), targets, sems = refs[:8], refs[8:11], refs[11:19], refs[19]
    copies = [pltpu.make_async_copy(a, b, sems.at[i]) for i, (a, b) in enumerate(zip(sources, targets))]
    for copy in copies:
        copy.start()
    for f, ref in enumerate(targets[:7]):
        copies[f].wait()
        strips(ref, e_ref, o_ref, T * (f // 2), 4 * (f % 2))
        if f in SHALLOW:
            i = SHALLOW.index(f)
            shallow_strips(ref, e_ref, o_ref, 4 * T + i, shallow, T * i)
    blank = jnp.zeros((T, 4, NZ), F32)
    e_ref[3 * T : 4 * T, 4:8, :] = blank
    o_ref[3 * T : 4 * T, 4:8, :] = blank
    copies[7].wait()


def beside_y(got, f, rows):
    odd = parity()[1] == 1
    slot, k = f // 2, 4 * (f % 2)
    a, b = (strip[rows(T * slot), k : k + 4, :] for strip in got)
    return jnp.where(odd, a, b), jnp.where(odd, b, a)


def shallow_beside_y(got, i):
    odd = parity()[1] == 1
    a, b = (strip[4 * T + i] for strip in got)
    return jnp.where(odd, a, b), jnp.where(odd, b, a)


def pack_x(*refs):
    fields, shallow, got, (e_ref, o_ref) = refs[:7], refs[7], refs[8:10], refs[10:]
    odd_x = parity()[0]
    for f, ref in enumerate(fields):
        width = WIDTHS[f]
        for low, out in ((odd_x, e_ref), (1 - odd_x, o_ref)):
            first = (1 - low) * (T - width)
            for i in range(width):
                x = first + i
                row = OFFSETS[f] + G * i
                below, above = beside_y(got, f, lambda start: start + x)
                out[row : row + 4, :] = below
                out[row + 4 : row + 20, :] = ref[x]
                out[row + 20 : row + 24, :] = above
    for i in range(len(SHALLOW)):
        row = SHALLOW_ROW + E * i
        below, above = shallow_beside_y(got, i)
        for out in (e_ref, o_ref):
            out[row : row + 8, :] = below
            out[row + 8 : row + 24, :] = shallow[T * i : T * i + T, :]
            out[row + 24 : row + 32, :] = above


def count_planes(wavelet, sx, sy, bits, rx, ry, src_ref, rec_ref, scale_ref):
    x0 = lax.axis_index("tx") * T - T
    y0 = lax.axis_index("ty") * T - H
    for t in range(STEPS):
        scale_ref[t : t + 1, :] = jnp.full((1, NZ), wavelet[t], F32)

    def rows(values):
        grid = lax.broadcasted_iota(jnp.int32, (E, values.shape[1]), 0) + y0
        return jnp.where(grid == values, 1.0, 0.0).astype(F32)

    dims = (((1,), (1,)), ((), ()))
    sign = (2 * bits[...] - 1).astype(F32)
    for values, ys, depth, weight, out in (
        (sx[...], sy[...], SRC_DEPTH, sign, src_ref),
        (rx[...], ry[...], REC_DEPTH, None, rec_ref),
    ):
        left = rows(ys)
        if weight is not None:
            left = left * weight
        grid = lax.broadcasted_iota(jnp.int32, (NZ, values.shape[1]), 0)
        here = grid % SH == depth
        for piece in range(3):
            hit = here & (grid // SH + (x0 + T * piece) == values)
            right = jnp.where(hit, 1.0, 0.0).astype(F32)
            out[piece] = lax.dot_general(left, right, dims, preferred_element_type=F32)


def laplace(ref, x, n, ys, ny):
    rows = pl.ds(x, n)
    lane = lanes((1, 1, NZ))
    center = ref[rows, pl.ds(ys, ny), :]
    total = ref[pl.ds(x + 1, n), pl.ds(ys, ny), :] + ref[pl.ds(x - 1, n), pl.ds(ys, ny), :]
    total = total + ref[rows, pl.ds(ys + 1, ny), :] + ref[rows, pl.ds(ys - 1, ny), :]
    down = jnp.where(lane == NZ - 1, 0.0, turn(center, -1))
    up = jnp.where(lane == 0, 0.0, turn(center, 1))
    return center, total + down + up - 6.0 * center


def shallow_laplace(ref):
    rows = pl.ds(PAD, E)
    lane = lanes((3, E, NZ))
    center = ref[:, rows, :]
    total = ref[:, pl.ds(PAD + 1, E), :] + ref[:, pl.ds(PAD - 1, E), :]
    total = total + jnp.where(lane % SH == SH - 1, 0.0, turn(center, -1))
    total = total + jnp.where(lane % SH == 0, 0.0, turn(center, 1))
    left = turn(center, SH)
    right = turn(center, -SH)
    none = jnp.zeros((1, E, NZ), F32)
    left = jnp.where(lane < SH, jnp.concatenate([none, left[0:2]], 0), left)
    right = jnp.where(lane >= NZ - SH, jnp.concatenate([right[1:3], none], 0), right)
    return center, total + left + right - 6.0 * center


def loop(start, blocks, n, body):
    for i in range(blocks):
        body(XO + start + i * n)


ALL_Y = pl.ds(PAD, G)
OWN_Y = pl.ds(PAD + D, T)
OWN_X = pl.ds(XO + D, T)
PLAN = ((0, 4, 6), (2, 5, 4), (3, 3, 6), (4, 4, 4))
WIDE = (G + 2 * XO, G + 2 * PAD, NZ)
FLAT = (G + 2 * XO, G, NZ)
LOW = (3, E + 2 * PAD, NZ)


def clear_ends(ref):
    blank = jnp.zeros((3, PAD, NZ), F32)
    ref[:, 0:PAD, :] = blank
    ref[:, PAD + E : PAD + E + PAD, :] = blank


def assemble(f, ref, ext, got, xe, xo):
    odd = parity()[0] == 1
    ext[OWN_X, OWN_Y, :] = ref[...]
    below, above = beside_y(got, f, lambda start: slice(start, start + T))
    ext[OWN_X, PAD : PAD + 4, :] = below
    ext[OWN_X, PAD + 20 : PAD + 24, :] = above
    width = WIDTHS[f]
    for i in range(width):
        rows = pl.ds(OFFSETS[f] + G * i, G)
        got_e = xe[rows, :]
        got_o = xo[rows, :]
        ext[XO + D - width + i, ALL_Y, :] = jnp.where(odd, got_e, got_o)
        ext[XO + D + T + i, ALL_Y, :] = jnp.where(odd, got_o, got_e)


def assemble_shallow(i, mine, ext, got, xe, xo):
    odd = parity()[0] == 1
    rows = pl.ds(SHALLOW_ROW + E * i, E)
    got_e = xe[rows, :]
    got_o = xo[rows, :]
    ext[0, PAD : PAD + E, :] = jnp.where(odd, got_e, got_o)
    ext[2, PAD : PAD + E, :] = jnp.where(odd, got_o, got_e)
    ext[1, PAD + H : PAD + H + T, :] = mine
    below, above = shallow_beside_y(got, i)
    ext[1, PAD : PAD + H, :] = below
    ext[1, PAD + H + T : PAD + E, :] = above


def background(x, n, scale, now, old, C, SF, t):
    rows = pl.ds(x, n)
    center, lap = laplace(now, x, n, PAD, G)
    accel = C[rows, ALL_Y, :] * lap + scale * SF[rows]
    if t < STEPS - 1:
        old[rows, ALL_Y, :] = 2.0 * center - old[rows, ALL_Y, :] + accel
    return accel


def place_sources(src, SF):
    short = lanes((G, NZ))
    for x in range(1, G - 1):
        piece, at = (x - D + T) // T, SH * ((x - D) % T)
        SF[XO + x] = jnp.where(short == SRC_DEPTH, turn(src[piece, 4:28, :], -at), 0.0)


def free(scales, *refs):
    fields, shallow, got, refs = refs[:7], refs[7], refs[8:10], refs[10:]
    xe, xo, src, SA, CS, BS0, BS1, first, second, IM = refs[:10]
    U0, U1, C, M0, M1, Q0, Q1, SF, A, US = refs[10:]
    rows = pl.ds(PAD, E)

    with jax.named_scope("assemble"):
        for f, ext in ((0, U0), (2, C), (3, M0), (4, U1), (6, M1)):
            assemble(f, fields[f], ext, got, xe, xo)
        for ext in (US.at[0], US.at[1], BS0, BS1):
            clear_ends(ext)
        for i, ext in enumerate((US.at[0], BS1, CS, US.at[1], BS0)):
            assemble_shallow(i, shallow[T * i : T * i + T, :], ext, got, xe, xo)
        place_sources(src, SF)

    with jax.named_scope("shallow"):
        for t in range(STEPS):
            now, old = US.at[t % 2], US.at[1 - t % 2]
            center, lap = shallow_laplace(now)
            accel = CS[:, rows, :] * lap + scales[t : t + 1, :][None] * src[...]
            SA[t] = accel
            if t < STEPS - 1:
                old[:, rows, :] = 2.0 * center - old[:, rows, :] + accel

    waves = (U1, U0)
    for t in range(STEPS):
        with jax.named_scope("forward"):
            old, now = waves
            scale = scales[t : t + 1, :][None]
            start, blocks, n = PLAN[t]

            def forward(x):
                A[t, pl.ds(x, n)] = background(x, n, scale, now, old, C, SF, t)

            loop(start, blocks, n, forward)
            waves = (now, old)

    def scaled(x):
        rows = pl.ds(x, 6)
        Q0[rows, ALL_Y, :] = C[rows, ALL_Y, :] * M0[rows, ALL_Y, :]

    loop(0, 4, 6, scaled)
    upcoming, latest, q_now, q_new = M0, M1, Q0, Q1
    for t in range(STEPS, 1, -1):
        with jax.named_scope("adjoint"):
            start, blocks, n = PLAN[STEPS - t]

            def back(x):
                rows = pl.ds(x, n)
                _, lap = laplace(q_now, x, n, PAD, G)
                current = 2.0 * upcoming[rows, ALL_Y, :] - latest[rows, ALL_Y, :] + lap
                latest[rows, ALL_Y, :] = current
                q_new[rows, ALL_Y, :] = C[rows, ALL_Y, :] * current

            loop(start, blocks, n, back)
            upcoming, latest = latest, upcoming
            q_now, q_new = q_new, q_now

            def gather(x):
                rows = pl.ds(x, 4)
                mine = pl.ds(x - XO - D, 4)
                product = A[t - 1, rows, D : D + T, :] * upcoming[rows, OWN_Y, :]
                IM[mine] = -product if t == STEPS else IM[mine] - product

            loop(D, 4, 4, gather)

    def finish(x):
        rows = pl.ds(x, 4)
        mine = pl.ds(x - XO - D, 4)
        _, lap = laplace(q_now, x, 4, PAD + D, T)
        ahead = upcoming[rows, OWN_Y, :]
        current = 2.0 * ahead - latest[rows, OWN_Y, :] + lap
        first[mine] = current
        second[mine] = ahead
        IM[mine] = IM[mine] - A[0, rows, D : D + T, :] * current

    loop(D, 4, 4, finish)


def meet(SA, CS, BS0, BS1, IM0, mine, got, rec, image, sent, BS, PS, QS, IM):
    rows = pl.ds(PAD, E)
    with jax.named_scope("turn"):
        core = parity()[0] == 1
        planes = [jnp.where(core, got[pl.ds(s, SH, stride=8), :], mine[pl.ds(s, SH, stride=8), :]) for s in range(8)]
        planes = jnp.concatenate(planes, 0)
        turned = jnp.concatenate([planes, jnp.zeros((64, NZ), F32)], 0).T
        parts = [turned[32 * g : 32 * g + 32, :] for g in range(4)]
        flat = lanes((E, NZ))
        PS[0] = turn(parts[0], 64)
        PS[1] = jnp.where(flat < 64, parts[1], turn(parts[2], 64))
        PS[2] = parts[3]

    with jax.named_scope("shallow"):
        for i in range(STEPS):
            clear_ends(BS.at[i])
        for i in range(2):
            clear_ends(QS.at[i])
        olds = (BS0, BS1, BS.at[0], BS.at[1], BS.at[2], BS.at[3])
        for t in range(STEPS):
            center, lap = shallow_laplace(olds[t + 1])
            olds[t + 2][:, rows, :] = (
                2.0 * center - olds[t][:, rows, :] + CS[:, rows, :] * lap - PS[...] * SA[t]
            )
        own = pl.ds(H, T)
        now = rec[...] * BS[3, :, rows, :]
        older = None
        delta = -SA[3, 1, own, :] * now[1, H : H + T, :]
        for t in (3, 2, 1):
            QS[t % 2, :, rows, :] = CS[:, rows, :] * now
            _, lap = shallow_laplace(QS.at[t % 2])
            new = 2.0 * now + lap + rec[...] * BS[t - 1, :, rows, :]
            if older is not None:
                new = new - older
            now, older = new, now
            delta = delta - SA[t - 1, 1, own, :] * now[1, H : H + T, :]
        sent[0] = now[1, H : H + T, :]
        sent[1] = older[1, H : H + T, :]

    with jax.named_scope("image"):
        here = lanes((T, NZ)) < SH
        for x in range(T):
            IM[x] = IM0[x] + jnp.where(here, turn(delta, -SH * x), 0.0)
        for half in range(2):
            turned = IM[8 * half : 8 * half + 8].reshape(128, NZ).T
            for shot in range(2):
                image[pl.ds(256 * shot + half, 128, stride=2), :] = turned


def born(scales, *refs):
    fields, got, refs = refs[:7], refs[7:9], refs[9:]
    xe, xo, src, near, far, first0, second0, sent, last, before, first, second, U0, U1, C, PT, B, SF = refs
    for f, ext in ((0, U0), (1, B.at[1]), (2, C), (4, U1), (5, B.at[0])):
        assemble(f, fields[f], ext, got, xe, xo)
    place_sources(src, SF)
    core = parity()[0] == 1
    for s in range(8):
        planes = []
        for k in range(4):
            rows = pl.ds(128 * k + s, T, stride=8)
            a, b = near[rows, :], far[rows, :]
            planes += [jnp.where(core, b, a), jnp.where(core, a, b)]
        turned = jnp.concatenate(planes, 0).T
        for g in range(4):
            PT[8 * g + s] = turned[32 * g : 32 * g + 32, :]
    waves = (U1, U0)
    for t in range(STEPS):
        old, now = waves
        scale = scales[t : t + 1, :][None]
        start, blocks, n = PLAN[t]

        def step(x):
            rows = pl.ds(x, n)
            accel = background(x, n, scale, now, old, C, SF, t)
            center, lap = laplace(B.at[t + 1], x, n, PAD, G)
            B[t + 2, rows, ALL_Y, :] = (
                2.0 * center - B[t, rows, ALL_Y, :] + C[rows, ALL_Y, :] * lap
                - PT[pl.ds(x - XO + 4, n), 4:28, :] * accel
            )

        loop(start, blocks, n, step)
        waves = (now, old)
    last[...] = B[STEPS + 1, OWN_X, OWN_Y, :]
    before[...] = B[STEPS, OWN_X, OWN_Y, :]
    here = lanes((T, NZ)) < SH
    for x in range(T):
        first[x] = first0[x] + jnp.where(here, turn(sent[0], -SH * x), 0.0)
        second[x] = second0[x] + jnp.where(here, turn(sent[1], -SH * x), 0.0)


def arrange(arrived, out):
    first = lax.axis_index("shot") * 16
    lane = lanes((8, NZ))
    for half in range(2):
        groups = []
        for j in range(8):
            groups.append(
                arrived[pl.ds(first + 2 * j + half, 8, stride=32), :]
                + arrived[pl.ds(first + 256 + 2 * j + half, 8, stride=32), :]
            )
        for k in range(8):
            line = jnp.zeros((8, NZ), F32)
            for j in range(8):
                line = jnp.where((lane >= 16 * j) & (lane < 16 * j + 16), turn(groups[j], 16 * j - 16 * k), line)
            out[pl.ds(8 * half + k, 8, stride=16), :] = line


def swap(cells, axis, odd):
    count = lax.axis_size(axis)
    pairs = [(i, ((i - odd) ^ 1) + odd) for i in range(odd, count - odd)]
    return lax.ppermute(cells, axis, pairs)


def per_device(
    perturbation, courant_sq, background_prev, background_now, born_prev, born_now,
    adjoint_next, adjoint_after, encode_bits, wavelet, source_x, source_y, receiver_x, receiver_y,
):
    shape = lambda *dims: jax.ShapeDtypeStruct(dims, F32)
    tile = (T, T, NZ)
    fields = [
        a.reshape(tile)
        for a in (background_now, born_now, courant_sq, adjoint_next, background_prev, born_prev, adjoint_after)
    ]

    strip = shape(*STRIP_Y)
    send_e, send_o, shallow, *fields, plane = call(
        pack_fields,
        (strip, strip, shape(5 * T, NZ)) + (shape(*tile),) * 7 + (shape(128, 256),),
        [HBM] * 8,
        [pltpu.SemaphoreType.DMA((8,))],
    )(*[pltpu.with_memory_space_constraint(a, pltpu.HBM) for a in (*fields, perturbation.reshape(128, 256))])
    got = (swap(send_e, "ty", 0), swap(send_o, "ty", 1))
    side = pltpu.VMEM((144, NZ), F32)
    blocks = call(pack_windows, shape(768, NZ), [VMEM], [side, side])(plane)
    groups = [[(2 * chip + core) * 16 + ty for chip in range(4) for ty in range(16)] for core in range(2)]
    windows = lax.all_to_all(
        blocks.reshape(192, 4, NZ), ("tx", "ty"), split_axis=0, concat_axis=0, tiled=True, axis_index_groups=groups
    ).reshape(768, NZ)
    pieces = shape(3, E, NZ)
    src, rec, scales = call(count_planes, (pieces, pieces, shape(8, NZ)), [SMEM] + [VMEM] * 5)(
        wavelet, source_x[None], source_y[None], encode_bits, receiver_x[None], receiver_y[None]
    )
    windows, src, rec, scales = lax.optimization_barrier((windows, src, rec, scales))
    near, other = call(split_windows, (shape(512, NZ), shape(512, NZ)), [VMEM])(windows)
    far = swap(other, "tx", 0)
    strip = shape(*STRIP_X)
    send_e, send_o = call(pack_x, (strip, strip), [VMEM] * 10, cost=BUSY)(*fields, shallow, *got)
    across = (swap(send_e, "tx", 0), swap(send_o, "tx", 1))
    one = lambda *dims: pltpu.VMEM(dims, F32)
    cells = shape(*tile)
    low = shape(*LOW)
    SA, CS, BS0, BS1, first, second, IM = call(
        free,
        (shape(STEPS, 3, E, NZ), low, low, low, cells, cells, cells),
        [VMEM] * 14,
        [one(*WIDE)] * 7 + [one(*FLAT), one(STEPS, *FLAT), one(2, *LOW)],
    )(scales, *fields, shallow, *got, *across, src)
    image, sent = call(
        meet,
        (shape(512, NZ), shape(2, T, NZ)),
        [VMEM] * 8,
        [one(4, *LOW), one(3, E, NZ), one(2, *LOW), one(*tile)],
    )(SA, CS, BS0, BS1, IM, near, far, rec)
    last, before, first, second = call(
        born,
        (cells, cells, cells, cells),
        [VMEM] * 18,
        [one(*WIDE)] * 3 + [one(E, E, NZ), one(STEPS + 2, *WIDE), one(*FLAT)],
    )(scales, *fields, *got, *across, src, near, far, first, second, sent)

    arrived = lax.all_to_all(
        image.reshape(256, 2, NZ), ("shot", "tx", "ty"), split_axis=0, concat_axis=0, tiled=True
    )
    hessian = call(arrange, shape(128, NZ), [VMEM])(arrived.reshape(512, NZ))
    return (hessian[None], first[None], second[None], last[None], before[None])


def solution(mesh):
    field = P("shot", "tx", "ty", None)
    placed = (
        P(("tx", "ty"), None, None),
        P("tx", "ty", None),
        field, field, field, field, field, field,
        P("shot", None),
        P(), P(), P(), P(), P(),
    )
    return jax.shard_map(
        per_device,
        mesh=mesh,
        in_specs=placed,
        out_specs=(P(("tx", "ty"), None, "shot"), field, field, field, field),
        check_vma=False,
    )
```

```python
import jax
import jax.numpy as jnp
from jax import lax
from jax.experimental import pallas as pl
from jax.experimental.pallas import tpu as pltpu
from jax.sharding import PartitionSpec as P

STEPS = 4
SRC_DEPTH = 4
REC_DEPTH = 2
NZ = 128
T = 16
D = 4
G = T + 2 * D
H = 8
E = T + 2 * H
PAD = 8
XO = 1
SH = 8
WIDTHS = (4, 4, 4, 4, 3, 3, 3)
OFFSETS = tuple(sum(WIDTHS[:i]) * G for i in range(len(WIDTHS)))
SHALLOW = (0, 1, 2, 4, 5)
SHALLOW_ROW = sum(WIDTHS) * G
STRIP_Y = (4 * T + 5, 8, NZ)
STRIP_X = (SHALLOW_ROW + len(SHALLOW) * E, NZ)
F32 = jnp.float32
VMEM = pl.BlockSpec(memory_space=pltpu.VMEM)
SMEM = pl.BlockSpec(memory_space=pltpu.SMEM)
HBM = pl.BlockSpec(memory_space=pltpu.HBM)


BUSY = pl.CostEstimate(flops=10**15, bytes_accessed=10**9, transcendentals=0)


def call(body, outs, specs, scratch=(), mib=20, cost=None, places=None):
    return pl.pallas_call(
        body,
        out_shape=outs,
        in_specs=specs,
        out_specs=places or jax.tree.map(lambda _: VMEM, outs),
        scratch_shapes=list(scratch),
        compiler_params=pltpu.CompilerParams(vmem_limit_bytes=mib * 1024 * 1024),
        cost_estimate=cost,
    )


def lanes(shape):
    return lax.broadcasted_iota(jnp.int32, shape, len(shape) - 1)


def turn(piece, amount):
    amount = amount % NZ
    return pltpu.roll(piece, amount, len(piece.shape) - 1) if amount else piece


def pack_windows(plane_ref, out_ref, left, right):
    lane = lanes((8, NZ))
    for half, side in enumerate((left, right)):
        side[0:8, :] = jnp.zeros((8, NZ), F32)
        side[136:160, :] = jnp.zeros((24, NZ), F32)
        side[8:136, :] = plane_ref[:, NZ * half : NZ * half + NZ]

    def put(block, row, start, at):
        for half, side in enumerate((left, right)):
            lo = max(start, NZ * half)
            hi = min(start + 32, NZ * half + NZ)
            if lo < hi:
                here = (lane >= at + lo - start) & (lane < at + hi - start)
                block = jnp.where(here, turn(side[8 + row : 16 + row, :], at - start), block)
        return block

    for chip in range(4):
        for ty in range(16):
            main = rest = jnp.zeros((8, NZ), F32)
            for g in range(4):
                main = put(main, 32 * chip - 6 + 8 * g, 16 * ty - 8, 32 * g)
                rest = put(rest, 32 * chip + 26 + 3 * g, 16 * ty - 8, 32 * g)
            row = 11 * (16 * chip + ty)
            out_ref[row : row + 8, :] = main
            out_ref[row + 8 : row + 11, :] = rest[0:3]


def split_windows(source, mine, other, arrived, sem):
    core = parity()[0] == 1
    lane = lanes((8, NZ))
    sub = lax.broadcasted_iota(jnp.int32, (8, NZ), 0)
    count = mine.shape[0] // 8
    copy = pltpu.make_async_copy(source.at[pl.ds(0, 11 * count)], arrived.at[pl.ds(0, 11 * count)], sem.at[0])
    copy.start()
    arrived[11 * count : 11 * count + 16, :] = jnp.zeros((16, NZ), F32)
    copy.wait()
    for k in range(count):
        row = 11 * k

        def rows(first):
            return arrived[row + first : row + first + 8, :]

        main = rows(0)
        third = jnp.where(sub < 3, turn(rows(8), 64), jnp.where(sub < 6, turn(rows(5), 32), rows(2)))
        fourth = jnp.where(sub < 1, turn(rows(10), 32), jnp.where(sub < 4, rows(7), 0.0))
        upper = jnp.where(lane < 64, turn(main, 64), jnp.where(lane < 96, third, fourth))
        mine[8 * k : 8 * k + 8, :] = jnp.where(core, upper, main)
        other[8 * k : 8 * k + 8, :] = jnp.where(core, main, upper)


def parity():
    return lax.rem(lax.axis_index("tx"), 2), lax.rem(lax.axis_index("ty"), 2)


def strips(ref, e_ref, o_ref, row, k):
    odd = parity()[1] == 1
    low = ref[:, 0:4, :]
    high = ref[:, 12:16, :]
    e_ref[row : row + T, k : k + 4, :] = jnp.where(odd, low, high)
    o_ref[row : row + T, k : k + 4, :] = jnp.where(odd, high, low)


def shallow_strips(ref, e_ref, o_ref, row, shallow, at):
    odd = parity()[1] == 1
    lane = lanes((T, NZ))
    packed = ref[0]
    for x in range(1, T):
        packed = jnp.where(lane >= SH * x, turn(ref[x], SH * x), packed)
    shallow[at : at + T, :] = packed
    e_ref[row] = jnp.where(odd, packed[0:8], packed[8:16])
    o_ref[row] = jnp.where(odd, packed[8:16], packed[0:8])


def pack_fields(*refs):
    sources, (e_ref, o_ref, shallow), targets, sems = refs[:8], refs[8:11], refs[11:19], refs[19]
    copies = [pltpu.make_async_copy(a, b, sems.at[i]) for i, (a, b) in enumerate(zip(sources, targets))]
    for copy in copies:
        copy.start()
    for f, ref in enumerate(targets[:7]):
        copies[f].wait()
        strips(ref, e_ref, o_ref, T * (f // 2), 4 * (f % 2))
        if f in SHALLOW:
            i = SHALLOW.index(f)
            shallow_strips(ref, e_ref, o_ref, 4 * T + i, shallow, T * i)
    blank = jnp.zeros((T, 4, NZ), F32)
    e_ref[3 * T : 4 * T, 4:8, :] = blank
    o_ref[3 * T : 4 * T, 4:8, :] = blank
    copies[7].wait()


def beside_y(got, f, rows):
    odd = parity()[1] == 1
    slot, k = f // 2, 4 * (f % 2)
    a, b = (strip[rows(T * slot), k : k + 4, :] for strip in got)
    return jnp.where(odd, a, b), jnp.where(odd, b, a)


def shallow_beside_y(got, i):
    odd = parity()[1] == 1
    a, b = (strip[4 * T + i] for strip in got)
    return jnp.where(odd, a, b), jnp.where(odd, b, a)


def pack_x(*refs):
    fields, shallow, got, (e_ref, o_ref) = refs[:7], refs[7], refs[8:10], refs[10:]
    odd_x = parity()[0]
    for f, ref in enumerate(fields):
        width = WIDTHS[f]
        for low, out in ((odd_x, e_ref), (1 - odd_x, o_ref)):
            first = (1 - low) * (T - width)
            for i in range(width):
                x = first + i
                row = OFFSETS[f] + G * i
                below, above = beside_y(got, f, lambda start: start + x)
                out[row : row + 4, :] = below
                out[row + 4 : row + 20, :] = ref[x]
                out[row + 20 : row + 24, :] = above
    for i in range(len(SHALLOW)):
        row = SHALLOW_ROW + E * i
        below, above = shallow_beside_y(got, i)
        for out in (e_ref, o_ref):
            out[row : row + 8, :] = below
            out[row + 8 : row + 24, :] = shallow[T * i : T * i + T, :]
            out[row + 24 : row + 32, :] = above


def count_planes(wavelet, sx, sy, bits, rx, ry, src_ref, rec_ref, scale_ref):
    x0 = lax.axis_index("tx") * T - T
    y0 = lax.axis_index("ty") * T - H
    for t in range(STEPS):
        scale_ref[t : t + 1, :] = jnp.full((1, NZ), wavelet[t], F32)

    def rows(values):
        grid = lax.broadcasted_iota(jnp.int32, (E, values.shape[1]), 0) + y0
        return jnp.where(grid == values, 1.0, 0.0).astype(F32)

    dims = (((1,), (1,)), ((), ()))
    sign = (2 * bits[...] - 1).astype(F32)
    for values, ys, depth, weight, out in (
        (sx[...], sy[...], SRC_DEPTH, sign, src_ref),
        (rx[...], ry[...], REC_DEPTH, None, rec_ref),
    ):
        left = rows(ys)
        if weight is not None:
            left = left * weight
        grid = lax.broadcasted_iota(jnp.int32, (NZ, values.shape[1]), 0)
        here = grid % SH == depth
        for piece in range(3):
            hit = here & (grid // SH + (x0 + T * piece) == values)
            right = jnp.where(hit, 1.0, 0.0).astype(F32)
            out[piece] = lax.dot_general(left, right, dims, preferred_element_type=F32)


def laplace(ref, x, n, ys, ny):
    rows = pl.ds(x, n)
    lane = lanes((1, 1, NZ))
    center = ref[rows, pl.ds(ys, ny), :]
    total = ref[pl.ds(x + 1, n), pl.ds(ys, ny), :] + ref[pl.ds(x - 1, n), pl.ds(ys, ny), :]
    total = total + ref[rows, pl.ds(ys + 1, ny), :] + ref[rows, pl.ds(ys - 1, ny), :]
    down = jnp.where(lane == NZ - 1, 0.0, turn(center, -1))
    up = jnp.where(lane == 0, 0.0, turn(center, 1))
    return center, total + down + up - 6.0 * center


def shallow_laplace(ref):
    rows = pl.ds(PAD, E)
    lane = lanes((3, E, NZ))
    center = ref[:, rows, :]
    total = ref[:, pl.ds(PAD + 1, E), :] + ref[:, pl.ds(PAD - 1, E), :]
    total = total + jnp.where(lane % SH == SH - 1, 0.0, turn(center, -1))
    total = total + jnp.where(lane % SH == 0, 0.0, turn(center, 1))
    left = turn(center, SH)
    right = turn(center, -SH)
    none = jnp.zeros((1, E, NZ), F32)
    left = jnp.where(lane < SH, jnp.concatenate([none, left[0:2]], 0), left)
    right = jnp.where(lane >= NZ - SH, jnp.concatenate([right[1:3], none], 0), right)
    return center, total + left + right - 6.0 * center


def loop(start, blocks, n, body):
    for i in range(blocks):
        body(XO + start + i * n)


ALL_Y = pl.ds(PAD, G)
OWN_Y = pl.ds(PAD + D, T)
OWN_X = pl.ds(XO + D, T)
PLAN = ((0, 4, 6), (2, 5, 4), (3, 3, 6), (4, 4, 4))
WIDE = (G + 2 * XO, G + 2 * PAD, NZ)
FLAT = (G + 2 * XO, G, NZ)
LOW = (3, E + 2 * PAD, NZ)


def clear_ends(ref):
    blank = jnp.zeros((3, PAD, NZ), F32)
    ref[:, 0:PAD, :] = blank
    ref[:, PAD + E : PAD + E + PAD, :] = blank


def assemble(f, ref, ext, got, xe, xo):
    odd = parity()[0] == 1
    ext[OWN_X, OWN_Y, :] = ref[...]
    below, above = beside_y(got, f, lambda start: slice(start, start + T))
    ext[OWN_X, PAD : PAD + 4, :] = below
    ext[OWN_X, PAD + 20 : PAD + 24, :] = above
    width = WIDTHS[f]
    for i in range(width):
        rows = pl.ds(OFFSETS[f] + G * i, G)
        got_e = xe[rows, :]
        got_o = xo[rows, :]
        ext[XO + D - width + i, ALL_Y, :] = jnp.where(odd, got_e, got_o)
        ext[XO + D + T + i, ALL_Y, :] = jnp.where(odd, got_o, got_e)


def assemble_shallow(i, mine, ext, got, xe, xo):
    odd = parity()[0] == 1
    rows = pl.ds(SHALLOW_ROW + E * i, E)
    got_e = xe[rows, :]
    got_o = xo[rows, :]
    ext[0, PAD : PAD + E, :] = jnp.where(odd, got_e, got_o)
    ext[2, PAD : PAD + E, :] = jnp.where(odd, got_o, got_e)
    ext[1, PAD + H : PAD + H + T, :] = mine
    below, above = shallow_beside_y(got, i)
    ext[1, PAD : PAD + H, :] = below
    ext[1, PAD + H + T : PAD + E, :] = above


def background(x, n, scale, now, old, C, SF, t):
    rows = pl.ds(x, n)
    center, lap = laplace(now, x, n, PAD, G)
    accel = C[rows, ALL_Y, :] * lap + scale * SF[rows]
    if t < STEPS - 1:
        old[rows, ALL_Y, :] = 2.0 * center - old[rows, ALL_Y, :] + accel
    return accel


def place_sources(src, SF):
    short = lanes((G, NZ))
    for x in range(1, G - 1):
        piece, at = (x - D + T) // T, SH * ((x - D) % T)
        SF[XO + x] = jnp.where(short == SRC_DEPTH, turn(src[piece, 4:28, :], -at), 0.0)


def free(scales, *refs):
    fields, shallow, got, refs = refs[:7], refs[7], refs[8:10], refs[10:]
    xe, xo, src, SA, CS, BS0, BS1, first, second, image = refs[:10]
    U0, U1, C, M0, M1, Q0, Q1, SF, A, US, IM = refs[10:]
    rows = pl.ds(PAD, E)

    with jax.named_scope("assemble"):
        for f, ext in ((0, U0), (2, C), (3, M0), (4, U1), (6, M1)):
            assemble(f, fields[f], ext, got, xe, xo)
        for ext in (US.at[0], US.at[1], BS0, BS1):
            clear_ends(ext)
        for i, ext in enumerate((US.at[0], BS1, CS, US.at[1], BS0)):
            assemble_shallow(i, shallow[T * i : T * i + T, :], ext, got, xe, xo)
        place_sources(src, SF)

    with jax.named_scope("shallow"):
        for t in range(STEPS):
            now, old = US.at[t % 2], US.at[1 - t % 2]
            center, lap = shallow_laplace(now)
            accel = CS[:, rows, :] * lap + scales[t : t + 1, :][None] * src[...]
            SA[t] = accel
            if t < STEPS - 1:
                old[:, rows, :] = 2.0 * center - old[:, rows, :] + accel

    waves = (U1, U0)
    for t in range(STEPS):
        with jax.named_scope("forward"):
            old, now = waves
            scale = scales[t : t + 1, :][None]
            start, blocks, n = PLAN[t]

            def forward(x):
                A[t, pl.ds(x, n)] = background(x, n, scale, now, old, C, SF, t)

            loop(start, blocks, n, forward)
            waves = (now, old)

    def scaled(x):
        rows = pl.ds(x, 6)
        Q0[rows, ALL_Y, :] = C[rows, ALL_Y, :] * M0[rows, ALL_Y, :]

    loop(0, 4, 6, scaled)
    upcoming, latest, q_now, q_new = M0, M1, Q0, Q1
    for t in range(STEPS, 1, -1):
        with jax.named_scope("adjoint"):
            start, blocks, n = PLAN[STEPS - t]

            def back(x):
                rows = pl.ds(x, n)
                _, lap = laplace(q_now, x, n, PAD, G)
                current = 2.0 * upcoming[rows, ALL_Y, :] - latest[rows, ALL_Y, :] + lap
                latest[rows, ALL_Y, :] = current
                q_new[rows, ALL_Y, :] = C[rows, ALL_Y, :] * current

            loop(start, blocks, n, back)
            upcoming, latest = latest, upcoming
            q_now, q_new = q_new, q_now

            def gather(x):
                rows = pl.ds(x, 4)
                mine = pl.ds(x - XO - D, 4)
                product = A[t - 1, rows, D : D + T, :] * upcoming[rows, OWN_Y, :]
                IM[mine] = -product if t == STEPS else IM[mine] - product

            loop(D, 4, 4, gather)

    def finish(x):
        rows = pl.ds(x, 4)
        mine = pl.ds(x - XO - D, 4)
        _, lap = laplace(q_now, x, 4, PAD + D, T)
        ahead = upcoming[rows, OWN_Y, :]
        current = 2.0 * ahead - latest[rows, OWN_Y, :] + lap
        first[mine] = current
        second[mine] = ahead
        IM[mine] = IM[mine] - A[0, rows, D : D + T, :] * current

    loop(D, 4, 4, finish)
    for half in range(2):
        image[pl.ds(half, 128, stride=2), :] = IM[8 * half : 8 * half + 8].reshape(128, NZ).T


def meet(SA, CS, BS0, BS1, free_image, mine, got, rec, image, sent, BS, PS, QS, low, sems):
    deep = [
        pltpu.make_async_copy(
            free_image.at[pl.ds(2 * SH, 256 - 2 * SH)],
            image.at[pl.ds(256 * shot + 2 * SH, 256 - 2 * SH)],
            sems.at[shot],
        )
        for shot in range(2)
    ]
    for copy in deep:
        copy.start()
    rows = pl.ds(PAD, E)
    with jax.named_scope("turn"):
        core = parity()[0] == 1
        planes = [jnp.where(core, got[pl.ds(s, SH, stride=8), :], mine[pl.ds(s, SH, stride=8), :]) for s in range(8)]
        planes = jnp.concatenate(planes, 0)
        turned = jnp.concatenate([planes, jnp.zeros((64, NZ), F32)], 0).T
        parts = [turned[32 * g : 32 * g + 32, :] for g in range(4)]
        flat = lanes((E, NZ))
        pairs = [jnp.where(flat < 64, parts[2 * i], turn(parts[2 * i + 1], 64)) for i in range(2)]
        at = SH * (T - 6)
        PS[0] = turn(pairs[0], at)
        PS[1] = jnp.where(flat < at, turn(pairs[0], at), turn(pairs[1], at))
        PS[2] = turn(pairs[1], at)

    with jax.named_scope("shallow"):
        for i in range(STEPS):
            clear_ends(BS.at[i])
        for i in range(2):
            clear_ends(QS.at[i])
        olds = (BS0, BS1, BS.at[0], BS.at[1], BS.at[2], BS.at[3])
        for t in range(STEPS):
            center, lap = shallow_laplace(olds[t + 1])
            olds[t + 2][:, rows, :] = (
                2.0 * center - olds[t][:, rows, :] + CS[:, rows, :] * lap - PS[...] * SA[t]
            )
        own = pl.ds(H, T)
        now = rec[...] * BS[3, :, rows, :]
        older = None
        delta = -SA[3, 1, own, :] * now[1, H : H + T, :]
        for t in (3, 2, 1):
            QS[t % 2, :, rows, :] = CS[:, rows, :] * now
            _, lap = shallow_laplace(QS.at[t % 2])
            new = 2.0 * now + lap + rec[...] * BS[t - 1, :, rows, :]
            if older is not None:
                new = new - older
            now, older = new, now
            delta = delta - SA[t - 1, 1, own, :] * now[1, H : H + T, :]
        sent[0] = now[1, H : H + T, :]
        sent[1] = older[1, H : H + T, :]

    with jax.named_scope("image"):
        turned = jnp.concatenate([delta, jnp.zeros((NZ - T, NZ), F32)], 0).T
        lane = lanes((SH, NZ))
        for half in range(2):
            line = jnp.zeros((SH, NZ), F32)
            for k in range(8):
                x = 8 * half + k
                piece = turn(turned[SH * x : SH * x + SH, :], 16 * k)
                line = jnp.where((lane >= 16 * k) & (lane < 16 * k + 16), piece, line)
            low[pl.ds(half, SH, stride=2), :] = free_image[pl.ds(half, SH, stride=2), :] + line
        shallow = [
            pltpu.make_async_copy(low, image.at[pl.ds(256 * shot, 2 * SH)], sems.at[2 + shot]) for shot in range(2)
        ]
        for copy in shallow:
            copy.start()
        for copy in (*deep, *shallow):
            copy.wait()


def born(scales, *refs):
    fields, got, refs = refs[:7], refs[7:9], refs[9:]
    xe, xo, src, near, far, first0, second0, sent, last, before, first, second, U0, U1, C, PT, B, SF = refs
    for f, ext in ((0, U0), (1, B.at[1]), (2, C), (4, U1), (5, B.at[0])):
        assemble(f, fields[f], ext, got, xe, xo)
    place_sources(src, SF)
    core = parity()[0] == 1
    for s in range(8):
        planes = []
        for k in range(4):
            rows = pl.ds(128 * k + s, T, stride=8)
            a, b = near[rows, :], far[rows, :]
            planes += [jnp.where(core, b, a), jnp.where(core, a, b)]
        turned = jnp.concatenate(planes, 0).T
        for g in range(4):
            PT[8 * g + s] = turned[32 * g : 32 * g + 32, :]
    waves = (U1, U0)
    for t in range(STEPS):
        old, now = waves
        scale = scales[t : t + 1, :][None]
        start, blocks, n = PLAN[t]

        def step(x):
            rows = pl.ds(x, n)
            accel = background(x, n, scale, now, old, C, SF, t)
            center, lap = laplace(B.at[t + 1], x, n, PAD, G)
            B[t + 2, rows, ALL_Y, :] = (
                2.0 * center - B[t, rows, ALL_Y, :] + C[rows, ALL_Y, :] * lap
                - PT[pl.ds(x - XO + 2, n), 4:28, :] * accel
            )

        loop(start, blocks, n, step)
        waves = (now, old)
    last[...] = B[STEPS + 1, OWN_X, OWN_Y, :]
    before[...] = B[STEPS, OWN_X, OWN_Y, :]
    here = lanes((T, NZ)) < SH
    for x in range(T):
        first[x] = first0[x] + jnp.where(here, turn(sent[0], -SH * x), 0.0)
        second[x] = second0[x] + jnp.where(here, turn(sent[1], -SH * x), 0.0)


def arrange(arrived, out):
    first = lax.axis_index("shot") * 16
    lane = lanes((8, NZ))
    for half in range(2):
        groups = []
        for j in range(8):
            groups.append(
                arrived[pl.ds(first + 2 * j + half, 8, stride=32), :]
                + arrived[pl.ds(first + 256 + 2 * j + half, 8, stride=32), :]
            )
        for k in range(8):
            line = jnp.zeros((8, NZ), F32)
            for j in range(8):
                line = jnp.where((lane >= 16 * j) & (lane < 16 * j + 16), turn(groups[j], 16 * j - 16 * k), line)
            out[pl.ds(8 * half + k, 8, stride=16), :] = line


def swap(cells, axis, odd):
    count = lax.axis_size(axis)
    pairs = [(i, ((i - odd) ^ 1) + odd) for i in range(odd, count - odd)]
    return lax.ppermute(cells, axis, pairs)


def per_device(
    perturbation, courant_sq, background_prev, background_now, born_prev, born_now,
    adjoint_next, adjoint_after, encode_bits, wavelet, source_x, source_y, receiver_x, receiver_y,
):
    shape = lambda *dims: jax.ShapeDtypeStruct(dims, F32)
    tile = (T, T, NZ)
    fields = [
        a.reshape(tile)
        for a in (background_now, born_now, courant_sq, adjoint_next, background_prev, born_prev, adjoint_after)
    ]

    strip = shape(*STRIP_Y)
    send_e, send_o, shallow, *fields, plane = call(
        pack_fields,
        (strip, strip, shape(5 * T, NZ)) + (shape(*tile),) * 7 + (shape(128, 256),),
        [HBM] * 8,
        [pltpu.SemaphoreType.DMA((8,))],
    )(*[pltpu.with_memory_space_constraint(a, pltpu.HBM) for a in (*fields, perturbation.reshape(128, 256))])
    got = (swap(send_e, "ty", 0), swap(send_o, "ty", 1))
    side = pltpu.VMEM((160, NZ), F32)
    blocks = call(pack_windows, shape(704, NZ), [VMEM], [side, side])(plane)
    groups = [[(2 * chip + core) * 16 + ty for chip in range(4) for ty in range(16)] for core in range(2)]
    windows = lax.all_to_all(
        blocks.reshape(704, 1, NZ), ("tx", "ty"), split_axis=0, concat_axis=0, tiled=True, axis_index_groups=groups
    ).reshape(704, NZ)
    pieces = shape(3, E, NZ)
    src, rec, scales = call(count_planes, (pieces, pieces, shape(8, NZ)), [SMEM] + [VMEM] * 5)(
        wavelet, source_x[None], source_y[None], encode_bits, receiver_x[None], receiver_y[None]
    )
    strip = shape(*STRIP_X)
    send_e, send_o = call(pack_x, (strip, strip), [VMEM] * 10, cost=BUSY)(*fields, shallow, *got)
    across = (swap(send_e, "tx", 0), swap(send_o, "tx", 1))
    one = lambda *dims: pltpu.VMEM(dims, F32)
    cells = shape(*tile)
    low = shape(*LOW)
    SA, CS, BS0, BS1, first, second, image = call(
        free,
        (shape(STEPS, 3, E, NZ), low, low, low, cells, cells, shape(256, NZ)),
        [VMEM] * 14,
        [one(*WIDE)] * 7 + [one(*FLAT), one(STEPS, *FLAT), one(2, *LOW), one(*tile)],
    )(scales, *fields, shallow, *got, *across, src)
    sems = lambda n: pltpu.SemaphoreType.DMA((n,))

    def split(windows, count):
        return call(split_windows, (shape(8 * count, NZ),) * 2, [HBM], [one(11 * count + 16, NZ), sems(1)])(
            pltpu.with_memory_space_constraint(windows, pltpu.HBM)
        )

    windows, src = lax.optimization_barrier((windows, src))
    near, other = split(windows, SH)
    far = swap(other, "tx", 0)
    image, sent = call(
        meet,
        (shape(512, NZ), shape(2, T, NZ)),
        [VMEM] * 8,
        [one(4, *LOW), one(3, E, NZ), one(2, *LOW), one(2 * SH, NZ), sems(4)],
        places=(HBM, VMEM),
    )(SA, CS, BS0, BS1, image, near, far, rec)
    windows, image = lax.optimization_barrier((windows, image))
    near, other = split(windows, 64)
    far = swap(other, "tx", 0)
    last, before, first, second = call(
        born,
        (cells, cells, cells, cells),
        [VMEM] * 18,
        [one(*WIDE)] * 3 + [one(E, E, NZ), one(STEPS + 2, *WIDE), one(*FLAT)],
    )(scales, *fields, *got, *across, src, near, far, first, second, sent)

    arrived = lax.all_to_all(
        image.reshape(256, 2, NZ), ("shot", "tx", "ty"), split_axis=0, concat_axis=0, tiled=True
    )
    hessian = call(arrange, shape(128, NZ), [VMEM])(arrived.reshape(512, NZ))
    return (hessian[None], first[None], second[None], last[None], before[None])


def solution(mesh):
    field = P("shot", "tx", "ty", None)
    placed = (
        P(("tx", "ty"), None, None),
        P("tx", "ty", None),
        field, field, field, field, field, field,
        P("shot", None),
        P(), P(), P(), P(), P(),
    )
    return jax.shard_map(
        per_device,
        mesh=mesh,
        in_specs=placed,
        out_specs=(P(("tx", "ty"), None, "shot"), field, field, field, field),
        check_vma=False,
    )
```

```python
import jax
import jax.numpy as jnp
from jax import lax
from jax.experimental import pallas as pl
from jax.experimental.pallas import tpu as pltpu
from jax.sharding import PartitionSpec as P

STEPS = 4
SRC_DEPTH = 4
REC_DEPTH = 2
NZ = 128
T = 16
D = 4
G = T + 2 * D
H = 8
E = T + 2 * H
PAD = 8
XO = 1
SH = 8
WIDTHS = (4, 4, 4, 4, 3, 3, 3)
LENGTHS = tuple(tuple(T + 2 * (w - 1 - q) for q in range(w)) for w in WIDTHS)
OFFSETS = tuple(
    tuple(sum(map(sum, LENGTHS[:f])) + sum(lengths[:q]) for q in range(len(lengths)))
    for f, lengths in enumerate(LENGTHS)
)
SHALLOW = (0, 1, 2, 4, 5)
SHALLOW_ROW = -(-sum(map(sum, LENGTHS)) // 8) * 8
STRIP_Y = (4 * T + 5, 8, NZ)
STRIP_X = (SHALLOW_ROW + len(SHALLOW) * E, NZ)
F32 = jnp.float32
VMEM = pl.BlockSpec(memory_space=pltpu.VMEM)
SMEM = pl.BlockSpec(memory_space=pltpu.SMEM)
HBM = pl.BlockSpec(memory_space=pltpu.HBM)


BUSY = pl.CostEstimate(flops=10**15, bytes_accessed=10**9, transcendentals=0)


def call(body, outs, specs, scratch=(), mib=20, cost=None, places=None):
    return pl.pallas_call(
        body,
        out_shape=outs,
        in_specs=specs,
        out_specs=places or jax.tree.map(lambda _: VMEM, outs),
        scratch_shapes=list(scratch),
        compiler_params=pltpu.CompilerParams(vmem_limit_bytes=mib * 1024 * 1024),
        cost_estimate=cost,
    )


def lanes(shape):
    return lax.broadcasted_iota(jnp.int32, shape, len(shape) - 1)


def turn(piece, amount):
    amount = amount % NZ
    return pltpu.roll(piece, amount, len(piece.shape) - 1) if amount else piece


def pack_windows(plane_ref, out_ref, left, right):
    lane = lanes((8, NZ))
    for half, side in enumerate((left, right)):
        side[0:8, :] = jnp.zeros((8, NZ), F32)
        side[136:160, :] = jnp.zeros((24, NZ), F32)
        side[8:136, :] = plane_ref[:, NZ * half : NZ * half + NZ]

    def put(block, row, start, at):
        for half, side in enumerate((left, right)):
            lo = max(start, NZ * half)
            hi = min(start + 32, NZ * half + NZ)
            if lo < hi:
                here = (lane >= at + lo - start) & (lane < at + hi - start)
                block = jnp.where(here, turn(side[8 + row : 16 + row, :], at - start), block)
        return block

    for chip in range(4):
        for ty in range(16):
            main = rest = jnp.zeros((8, NZ), F32)
            for g in range(4):
                main = put(main, 32 * chip - 6 + 8 * g, 16 * ty - 8, 32 * g)
                rest = put(rest, 32 * chip + 26 + 3 * g, 16 * ty - 8, 32 * g)
            row = 11 * (16 * chip + ty)
            out_ref[row : row + 8, :] = main
            out_ref[row + 8 : row + 11, :] = rest[0:3]


def split_windows(source, mine, other, arrived, sem):
    core = parity()[0] == 1
    lane = lanes((8, NZ))
    sub = lax.broadcasted_iota(jnp.int32, (8, NZ), 0)
    count = mine.shape[0] // 8
    copy = pltpu.make_async_copy(source.at[pl.ds(0, 11 * count)], arrived.at[pl.ds(0, 11 * count)], sem.at[0])
    copy.start()
    arrived[11 * count : 11 * count + 16, :] = jnp.zeros((16, NZ), F32)
    copy.wait()
    for k in range(count):
        row = 11 * k

        def rows(first):
            return arrived[row + first : row + first + 8, :]

        main = rows(0)
        third = jnp.where(sub < 3, turn(rows(8), 64), jnp.where(sub < 6, turn(rows(5), 32), rows(2)))
        fourth = jnp.where(sub < 1, turn(rows(10), 32), jnp.where(sub < 4, rows(7), 0.0))
        upper = jnp.where(lane < 64, turn(main, 64), jnp.where(lane < 96, third, fourth))
        mine[8 * k : 8 * k + 8, :] = jnp.where(core, upper, main)
        other[8 * k : 8 * k + 8, :] = jnp.where(core, main, upper)


def parity():
    return lax.rem(lax.axis_index("tx"), 2), lax.rem(lax.axis_index("ty"), 2)


def strips(ref, e_ref, o_ref, row, k):
    odd = parity()[1] == 1
    low = ref[:, 0:4, :]
    high = ref[:, 12:16, :]
    e_ref[row : row + T, k : k + 4, :] = jnp.where(odd, low, high)
    o_ref[row : row + T, k : k + 4, :] = jnp.where(odd, high, low)


def shallow_strips(ref, e_ref, o_ref, row, shallow, at):
    odd = parity()[1] == 1
    lane = lanes((T, NZ))
    packed = ref[0]
    for x in range(1, T):
        packed = jnp.where(lane >= SH * x, turn(ref[x], SH * x), packed)
    shallow[at : at + T, :] = packed
    e_ref[row] = jnp.where(odd, packed[0:8], packed[8:16])
    o_ref[row] = jnp.where(odd, packed[8:16], packed[0:8])


def pack_fields(*refs):
    sources, (e_ref, o_ref, shallow), targets, sems = refs[:8], refs[8:11], refs[11:19], refs[19]
    copies = [pltpu.make_async_copy(a, b, sems.at[i]) for i, (a, b) in enumerate(zip(sources, targets))]
    for copy in copies:
        copy.start()
    for f, ref in enumerate(targets[:7]):
        copies[f].wait()
        strips(ref, e_ref, o_ref, T * (f // 2), 4 * (f % 2))
        if f in SHALLOW:
            i = SHALLOW.index(f)
            shallow_strips(ref, e_ref, o_ref, 4 * T + i, shallow, T * i)
    blank = jnp.zeros((T, 4, NZ), F32)
    e_ref[3 * T : 4 * T, 4:8, :] = blank
    o_ref[3 * T : 4 * T, 4:8, :] = blank
    copies[7].wait()


def beside_y(got, f, rows):
    odd = parity()[1] == 1
    slot, k = f // 2, 4 * (f % 2)
    a, b = (strip[rows(T * slot), k : k + 4, :] for strip in got)
    return jnp.where(odd, a, b), jnp.where(odd, b, a)


def shallow_beside_y(got, i):
    odd = parity()[1] == 1
    a, b = (strip[4 * T + i] for strip in got)
    return jnp.where(odd, a, b), jnp.where(odd, b, a)


def pack_x(*refs):
    fields, shallow, got, (e_ref, o_ref) = refs[:7], refs[7], refs[8:10], refs[10:]
    odd_x = parity()[0]
    for f, ref in enumerate(fields):
        width = WIDTHS[f]
        for low, out in ((odd_x, e_ref), (1 - odd_x, o_ref)):
            for q in range(width):
                x = low * q + (1 - low) * (T - 1 - q)
                row, more = OFFSETS[f][q], width - 1 - q
                if more:
                    below, above = beside_y(got, f, lambda start: start + x)
                    out[row : row + more, :] = below[4 - more : 4]
                    out[row + more + T : row + more + T + more, :] = above[0:more]
                out[row + more : row + more + T, :] = ref[x]
    for i in range(len(SHALLOW)):
        row = SHALLOW_ROW + E * i
        below, above = shallow_beside_y(got, i)
        for out in (e_ref, o_ref):
            out[row : row + 8, :] = below
            out[row + 8 : row + 24, :] = shallow[T * i : T * i + T, :]
            out[row + 24 : row + 32, :] = above


def count_planes(wavelet, sx, sy, bits, rx, ry, src_ref, rec_ref, scale_ref):
    x0 = lax.axis_index("tx") * T - T
    y0 = lax.axis_index("ty") * T - H
    for t in range(STEPS):
        scale_ref[t : t + 1, :] = jnp.full((1, NZ), wavelet[t], F32)

    def rows(values):
        grid = lax.broadcasted_iota(jnp.int32, (E, values.shape[1]), 0) + y0
        return jnp.where(grid == values, 1.0, 0.0).astype(F32)

    dims = (((1,), (1,)), ((), ()))
    sign = (2 * bits[...] - 1).astype(F32)
    for values, ys, depth, weight, out in (
        (sx[...], sy[...], SRC_DEPTH, sign, src_ref),
        (rx[...], ry[...], REC_DEPTH, None, rec_ref),
    ):
        left = rows(ys)
        if weight is not None:
            left = left * weight
        grid = lax.broadcasted_iota(jnp.int32, (NZ, values.shape[1]), 0)
        here = grid % SH == depth
        for piece in range(3):
            hit = here & (grid // SH + (x0 + T * piece) == values)
            right = jnp.where(hit, 1.0, 0.0).astype(F32)
            out[piece] = lax.dot_general(left, right, dims, preferred_element_type=F32)


def laplace(ref, x, n, ys, ny):
    rows = pl.ds(x, n)
    lane = lanes((1, 1, NZ))
    center = ref[rows, pl.ds(ys, ny), :]
    total = ref[pl.ds(x + 1, n), pl.ds(ys, ny), :] + ref[pl.ds(x - 1, n), pl.ds(ys, ny), :]
    total = total + ref[rows, pl.ds(ys + 1, ny), :] + ref[rows, pl.ds(ys - 1, ny), :]
    down = jnp.where(lane == NZ - 1, 0.0, turn(center, -1))
    up = jnp.where(lane == 0, 0.0, turn(center, 1))
    return center, total + down + up - 6.0 * center


def shallow_laplace(ref):
    rows = pl.ds(PAD, E)
    lane = lanes((1, 1, NZ))
    depth = lane & (SH - 1)
    center = ref[:, rows, :]
    total = ref[:, pl.ds(PAD + 1, E), :] + ref[:, pl.ds(PAD - 1, E), :]
    total = total + jnp.where(depth == SH - 1, 0.0, turn(center, -1))
    total = total + jnp.where(depth == 0, 0.0, turn(center, 1))
    left = turn(center, SH)
    right = turn(center, -SH)
    none = jnp.zeros((1, E, NZ), F32)
    left = jnp.where(lane < SH, jnp.concatenate([none, left[0:2]], 0), left)
    right = jnp.where(lane >= NZ - SH, jnp.concatenate([right[1:3], none], 0), right)
    return center, total + left + right - 6.0 * center


def loop(start, blocks, n, body):
    for i in range(blocks):
        body(XO + start + i * n)


ALL_Y = pl.ds(PAD, G)
OWN_Y = pl.ds(PAD + D, T)
OWN_X = pl.ds(XO + D, T)
PLAN = ((0, 4, 6), (2, 5, 4), (3, 3, 6), (4, 4, 4))
WIDE = (G + 2 * XO, G + 2 * PAD, NZ)
FLAT = (G + 2 * XO, G, NZ)
LOW = (3, E + 2 * PAD, NZ)


def clear_ends(ref):
    blank = jnp.zeros((3, PAD, NZ), F32)
    ref[:, 0:PAD, :] = blank
    ref[:, PAD + E : PAD + E + PAD, :] = blank


def assemble(f, ref, ext, got, xe, xo):
    odd = parity()[0] == 1
    ext[OWN_X, OWN_Y, :] = ref[...]
    below, above = beside_y(got, f, lambda start: slice(start, start + T))
    ext[OWN_X, PAD : PAD + 4, :] = below
    ext[OWN_X, PAD + 20 : PAD + 24, :] = above
    for q, length in enumerate(LENGTHS[f]):
        rows = pl.ds(OFFSETS[f][q], length)
        at = pl.ds(PAD + D - (length - T) // 2, length)
        got_e = xe[rows, :]
        got_o = xo[rows, :]
        ext[XO + D - 1 - q, at, :] = jnp.where(odd, got_e, got_o)
        ext[XO + D + T + q, at, :] = jnp.where(odd, got_o, got_e)


def assemble_shallow(i, mine, ext, got, xe, xo):
    odd = parity()[0] == 1
    rows = pl.ds(SHALLOW_ROW + E * i, E)
    got_e = xe[rows, :]
    got_o = xo[rows, :]
    ext[0, PAD : PAD + E, :] = jnp.where(odd, got_e, got_o)
    ext[2, PAD : PAD + E, :] = jnp.where(odd, got_o, got_e)
    ext[1, PAD + H : PAD + H + T, :] = mine
    below, above = shallow_beside_y(got, i)
    ext[1, PAD : PAD + H, :] = below
    ext[1, PAD + H + T : PAD + E, :] = above


def background(x, n, scale, now, old, C, SF, t):
    rows = pl.ds(x, n)
    center, lap = laplace(now, x, n, PAD, G)
    accel = C[rows, ALL_Y, :] * lap + scale * SF[rows]
    if t < STEPS - 1:
        old[rows, ALL_Y, :] = 2.0 * center - old[rows, ALL_Y, :] + accel
    return accel


def place_sources(src, SF):
    short = lanes((G, NZ))
    for x in range(1, G - 1):
        piece, at = (x - D + T) // T, SH * ((x - D) % T)
        SF[XO + x] = jnp.where(short == SRC_DEPTH, turn(src[piece, 4:28, :], -at), 0.0)


def free(scales, *refs):
    fields, shallow, got, refs = refs[:7], refs[7], refs[8:10], refs[10:]
    xe, xo, src, SA, CS, BS0, BS1, first, second, image = refs[:10]
    U0, U1, C, M0, M1, Q0, Q1, SF, A, US, IM = refs[10:]
    rows = pl.ds(PAD, E)

    with jax.named_scope("assemble"):
        for f, ext in ((0, U0), (2, C), (3, M0), (4, U1), (6, M1)):
            assemble(f, fields[f], ext, got, xe, xo)
        for ext in (US.at[0], US.at[1], BS0, BS1):
            clear_ends(ext)
        for i, ext in enumerate((US.at[0], BS1, CS, US.at[1], BS0)):
            assemble_shallow(i, shallow[T * i : T * i + T, :], ext, got, xe, xo)
        place_sources(src, SF)

    with jax.named_scope("shallow"):
        for t in range(STEPS):
            now, old = US.at[t % 2], US.at[1 - t % 2]
            center, lap = shallow_laplace(now)
            accel = CS[:, rows, :] * lap + scales[t : t + 1, :][None] * src[...]
            SA[t] = accel
            if t < STEPS - 1:
                old[:, rows, :] = 2.0 * center - old[:, rows, :] + accel

    waves = (U1, U0)
    for t in range(STEPS):
        with jax.named_scope("forward"):
            old, now = waves
            scale = scales[t : t + 1, :][None]
            start, blocks, n = PLAN[t]

            def forward(x):
                A[t, pl.ds(x, n)] = background(x, n, scale, now, old, C, SF, t)

            loop(start, blocks, n, forward)
            waves = (now, old)

    def scaled(x):
        rows = pl.ds(x, 6)
        Q0[rows, ALL_Y, :] = C[rows, ALL_Y, :] * M0[rows, ALL_Y, :]

    loop(0, 4, 6, scaled)
    upcoming, latest, q_now, q_new = M0, M1, Q0, Q1
    for t in range(STEPS, 1, -1):
        with jax.named_scope("adjoint"):
            start, blocks, n = PLAN[STEPS - t]

            def back(x):
                rows = pl.ds(x, n)
                _, lap = laplace(q_now, x, n, PAD, G)
                current = 2.0 * upcoming[rows, ALL_Y, :] - latest[rows, ALL_Y, :] + lap
                latest[rows, ALL_Y, :] = current
                q_new[rows, ALL_Y, :] = C[rows, ALL_Y, :] * current

            loop(start, blocks, n, back)
            upcoming, latest = latest, upcoming
            q_now, q_new = q_new, q_now

            def gather(x):
                rows = pl.ds(x, 4)
                mine = pl.ds(x - XO - D, 4)
                product = A[t - 1, rows, D : D + T, :] * upcoming[rows, OWN_Y, :]
                IM[mine] = -product if t == STEPS else IM[mine] - product

            loop(D, 4, 4, gather)

    def finish(x):
        rows = pl.ds(x, 4)
        mine = pl.ds(x - XO - D, 4)
        _, lap = laplace(q_now, x, 4, PAD + D, T)
        ahead = upcoming[rows, OWN_Y, :]
        current = 2.0 * ahead - latest[rows, OWN_Y, :] + lap
        first[mine] = current
        second[mine] = ahead
        IM[mine] = IM[mine] - A[0, rows, D : D + T, :] * current

    loop(D, 4, 4, finish)
    for half in range(2):
        image[pl.ds(half, 128, stride=2), :] = IM[8 * half : 8 * half + 8].reshape(128, NZ).T


def meet(SA, CS, BS0, BS1, free_image, mine, got, rec, image, sent, BS, PS, QS, low, sems):
    deep = [
        pltpu.make_async_copy(
            free_image.at[pl.ds(2 * SH, 256 - 2 * SH)],
            image.at[pl.ds(256 * shot + 2 * SH, 256 - 2 * SH)],
            sems.at[shot],
        )
        for shot in range(2)
    ]
    for copy in deep:
        copy.start()
    rows = pl.ds(PAD, E)
    with jax.named_scope("turn"):
        core = parity()[0] == 1
        planes = [jnp.where(core, got[pl.ds(s, SH, stride=8), :], mine[pl.ds(s, SH, stride=8), :]) for s in range(8)]
        planes = jnp.concatenate(planes, 0)
        turned = jnp.concatenate([planes, jnp.zeros((64, NZ), F32)], 0).T
        parts = [turned[32 * g : 32 * g + 32, :] for g in range(4)]
        flat = lanes((E, NZ))
        pairs = [jnp.where(flat < 64, parts[2 * i], turn(parts[2 * i + 1], 64)) for i in range(2)]
        at = SH * (T - 6)
        PS[0] = turn(pairs[0], at)
        PS[1] = jnp.where(flat < at, turn(pairs[0], at), turn(pairs[1], at))
        PS[2] = turn(pairs[1], at)

    with jax.named_scope("shallow"):
        for i in range(STEPS):
            clear_ends(BS.at[i])
        for i in range(2):
            clear_ends(QS.at[i])
        olds = (BS0, BS1, BS.at[0], BS.at[1], BS.at[2], BS.at[3])
        for t in range(STEPS):
            center, lap = shallow_laplace(olds[t + 1])
            olds[t + 2][:, rows, :] = (
                2.0 * center - olds[t][:, rows, :] + CS[:, rows, :] * lap - PS[...] * SA[t]
            )
        own = pl.ds(H, T)
        now = rec[...] * BS[3, :, rows, :]
        older = None
        delta = -SA[3, 1, own, :] * now[1, H : H + T, :]
        for t in (3, 2, 1):
            QS[t % 2, :, rows, :] = CS[:, rows, :] * now
            _, lap = shallow_laplace(QS.at[t % 2])
            new = 2.0 * now + lap + rec[...] * BS[t - 1, :, rows, :]
            if older is not None:
                new = new - older
            now, older = new, now
            delta = delta - SA[t - 1, 1, own, :] * now[1, H : H + T, :]
        sent[0] = now[1, H : H + T, :]
        sent[1] = older[1, H : H + T, :]

    with jax.named_scope("image"):
        turned = jnp.concatenate([delta, jnp.zeros((NZ - T, NZ), F32)], 0).T
        lane = lanes((SH, NZ))
        for half in range(2):
            line = jnp.zeros((SH, NZ), F32)
            for k in range(8):
                x = 8 * half + k
                piece = turn(turned[SH * x : SH * x + SH, :], 16 * k)
                line = jnp.where((lane >= 16 * k) & (lane < 16 * k + 16), piece, line)
            low[pl.ds(half, SH, stride=2), :] = free_image[pl.ds(half, SH, stride=2), :] + line
        shallow = [
            pltpu.make_async_copy(low, image.at[pl.ds(256 * shot, 2 * SH)], sems.at[2 + shot]) for shot in range(2)
        ]
        for copy in shallow:
            copy.start()
        for copy in (*deep, *shallow):
            copy.wait()


def born(scales, *refs):
    fields, got, refs = refs[:7], refs[7:9], refs[9:]
    xe, xo, src, near, far, first0, second0, sent, last, before, first, second, U0, U1, C, PT, B, SF = refs
    for f, ext in ((0, U0), (1, B.at[1]), (2, C), (4, U1), (5, B.at[0])):
        assemble(f, fields[f], ext, got, xe, xo)
    place_sources(src, SF)
    core = parity()[0] == 1
    for s in range(8):
        planes = []
        for k in range(4):
            rows = pl.ds(128 * k + s, T, stride=8)
            a, b = near[rows, :], far[rows, :]
            planes += [jnp.where(core, b, a), jnp.where(core, a, b)]
        turned = jnp.concatenate(planes, 0).T
        for g in range(4):
            PT[8 * g + s] = turned[32 * g : 32 * g + 32, :]
    waves = (U1, U0)
    for t in range(STEPS):
        old, now = waves
        scale = scales[t : t + 1, :][None]
        start, blocks, n = PLAN[t]

        def step(x):
            rows = pl.ds(x, n)
            accel = background(x, n, scale, now, old, C, SF, t)
            center, lap = laplace(B.at[t + 1], x, n, PAD, G)
            B[t + 2, rows, ALL_Y, :] = (
                2.0 * center - B[t, rows, ALL_Y, :] + C[rows, ALL_Y, :] * lap
                - PT[pl.ds(x - XO + 2, n), 4:28, :] * accel
            )

        loop(start, blocks, n, step)
        waves = (now, old)
    last[...] = B[STEPS + 1, OWN_X, OWN_Y, :]
    before[...] = B[STEPS, OWN_X, OWN_Y, :]
    here = lanes((T, NZ)) < SH
    for x in range(T):
        first[x] = first0[x] + jnp.where(here, turn(sent[0], -SH * x), 0.0)
        second[x] = second0[x] + jnp.where(here, turn(sent[1], -SH * x), 0.0)


def arrange(arrived, out):
    first = lax.axis_index("shot") * 16
    lane = lanes((8, NZ))
    for half in range(2):
        groups = []
        for j in range(8):
            groups.append(
                arrived[pl.ds(first + 2 * j + half, 8, stride=32), :]
                + arrived[pl.ds(first + 256 + 2 * j + half, 8, stride=32), :]
            )
        for k in range(8):
            line = jnp.zeros((8, NZ), F32)
            for j in range(8):
                line = jnp.where((lane >= 16 * j) & (lane < 16 * j + 16), turn(groups[j], 16 * j - 16 * k), line)
            out[pl.ds(8 * half + k, 8, stride=16), :] = line


def swap(cells, axis, odd):
    count = lax.axis_size(axis)
    pairs = [(i, ((i - odd) ^ 1) + odd) for i in range(odd, count - odd)]
    return lax.ppermute(cells, axis, pairs)


def per_device(
    perturbation, courant_sq, background_prev, background_now, born_prev, born_now,
    adjoint_next, adjoint_after, encode_bits, wavelet, source_x, source_y, receiver_x, receiver_y,
):
    shape = lambda *dims: jax.ShapeDtypeStruct(dims, F32)
    tile = (T, T, NZ)
    fields = [
        a.reshape(tile)
        for a in (background_now, born_now, courant_sq, adjoint_next, background_prev, born_prev, adjoint_after)
    ]

    strip = shape(*STRIP_Y)
    send_e, send_o, shallow, *fields, plane = call(
        pack_fields,
        (strip, strip, shape(5 * T, NZ)) + (shape(*tile),) * 7 + (shape(128, 256),),
        [HBM] * 8,
        [pltpu.SemaphoreType.DMA((8,))],
    )(*[pltpu.with_memory_space_constraint(a, pltpu.HBM) for a in (*fields, perturbation.reshape(128, 256))])
    got = (swap(send_e, "ty", 0), swap(send_o, "ty", 1))
    side = pltpu.VMEM((160, NZ), F32)
    blocks = call(pack_windows, shape(704, NZ), [VMEM], [side, side])(plane)
    groups = [[(2 * chip + core) * 16 + ty for chip in range(4) for ty in range(16)] for core in range(2)]
    windows = lax.all_to_all(
        blocks.reshape(704, 1, NZ), ("tx", "ty"), split_axis=0, concat_axis=0, tiled=True, axis_index_groups=groups
    ).reshape(704, NZ)
    pieces = shape(3, E, NZ)
    src, rec, scales = call(count_planes, (pieces, pieces, shape(8, NZ)), [SMEM] + [VMEM] * 5)(
        wavelet, source_x[None], source_y[None], encode_bits, receiver_x[None], receiver_y[None]
    )
    strip = shape(*STRIP_X)
    send_e, send_o = call(pack_x, (strip, strip), [VMEM] * 10, cost=BUSY)(*fields, shallow, *got)
    across = (swap(send_e, "tx", 0), swap(send_o, "tx", 1))
    one = lambda *dims: pltpu.VMEM(dims, F32)
    cells = shape(*tile)
    low = shape(*LOW)
    SA, CS, BS0, BS1, first, second, image = call(
        free,
        (shape(STEPS, 3, E, NZ), low, low, low, cells, cells, shape(256, NZ)),
        [VMEM] * 14,
        [one(*WIDE)] * 7 + [one(*FLAT), one(STEPS, *FLAT), one(2, *LOW), one(*tile)],
    )(scales, *fields, shallow, *got, *across, src)
    sems = lambda n: pltpu.SemaphoreType.DMA((n,))

    def split(windows, count):
        return call(split_windows, (shape(8 * count, NZ),) * 2, [HBM], [one(11 * count + 16, NZ), sems(1)])(
            pltpu.with_memory_space_constraint(windows, pltpu.HBM)
        )

    windows, src = lax.optimization_barrier((windows, src))
    near, other = split(windows, SH)
    far = swap(other, "tx", 0)
    image, sent = call(
        meet,
        (shape(512, NZ), shape(2, T, NZ)),
        [VMEM] * 8,
        [one(4, *LOW), one(3, E, NZ), one(2, *LOW), one(2 * SH, NZ), sems(4)],
        places=(HBM, VMEM),
    )(SA, CS, BS0, BS1, image, near, far, rec)
    windows, image = lax.optimization_barrier((windows, image))
    near, other = split(windows, 64)
    far = swap(other, "tx", 0)
    last, before, first, second = call(
        born,
        (cells, cells, cells, cells),
        [VMEM] * 18,
        [one(*WIDE)] * 3 + [one(E, E, NZ), one(STEPS + 2, *WIDE), one(*FLAT)],
    )(scales, *fields, *got, *across, src, near, far, first, second, sent)

    arrived = lax.all_to_all(
        image.reshape(256, 2, NZ), ("shot", "tx", "ty"), split_axis=0, concat_axis=0, tiled=True
    )
    hessian = call(arrange, shape(128, NZ), [VMEM])(arrived.reshape(512, NZ))
    return (hessian[None], first[None], second[None], last[None], before[None])


def solution(mesh):
    field = P("shot", "tx", "ty", None)
    placed = (
        P(("tx", "ty"), None, None),
        P("tx", "ty", None),
        field, field, field, field, field, field,
        P("shot", None),
        P(), P(), P(), P(), P(),
    )
    return jax.shard_map(
        per_device,
        mesh=mesh,
        in_specs=placed,
        out_specs=(P(("tx", "ty"), None, "shot"), field, field, field, field),
        check_vma=False,
    )
```

```python
import jax
import jax.numpy as jnp
from jax import lax
from jax.experimental import pallas as pl
from jax.experimental.pallas import tpu as pltpu
from jax.sharding import PartitionSpec as P

STEPS = 4
SRC_DEPTH = 4
REC_DEPTH = 2
NZ = 128
T = 16
D = 4
G = T + 2 * D
H = 8
E = T + 2 * H
PAD = 8
XO = 1
SH = 8
WIDTHS = (4, 4, 4, 4, 3, 3, 3)
LENGTHS = tuple(tuple(T + 2 * (w - 1 - q) for q in range(w)) for w in WIDTHS)
OFFSETS = tuple(
    tuple(sum(map(sum, LENGTHS[:f])) + sum(lengths[:q]) for q in range(len(lengths)))
    for f, lengths in enumerate(LENGTHS)
)
SHALLOW = (0, 1, 2, 4, 5)
SHALLOW_ROW = -(-sum(map(sum, LENGTHS)) // 8) * 8
STRIP_Y = (4 * T + 5, 8, NZ)
STRIP_X = (SHALLOW_ROW + len(SHALLOW) * E, NZ)
F32 = jnp.float32
VMEM = pl.BlockSpec(memory_space=pltpu.VMEM)
SMEM = pl.BlockSpec(memory_space=pltpu.SMEM)
HBM = pl.BlockSpec(memory_space=pltpu.HBM)


BUSY = pl.CostEstimate(flops=10**15, bytes_accessed=10**9, transcendentals=0)


def call(body, outs, specs, scratch=(), mib=20, cost=None, places=None):
    return pl.pallas_call(
        body,
        out_shape=outs,
        in_specs=specs,
        out_specs=places or jax.tree.map(lambda _: VMEM, outs),
        scratch_shapes=list(scratch),
        compiler_params=pltpu.CompilerParams(vmem_limit_bytes=mib * 1024 * 1024),
        cost_estimate=cost,
    )


def lanes(shape):
    return lax.broadcasted_iota(jnp.int32, shape, len(shape) - 1)


def turn(piece, amount):
    amount = amount % NZ
    return pltpu.roll(piece, amount, len(piece.shape) - 1) if amount else piece


def pack_windows(plane_ref, out_ref, left, right):
    lane = lanes((8, NZ))
    for half, side in enumerate((left, right)):
        side[0:8, :] = jnp.zeros((8, NZ), F32)
        side[136:160, :] = jnp.zeros((24, NZ), F32)
        side[8:136, :] = plane_ref[:, NZ * half : NZ * half + NZ]

    def put(block, row, start, at):
        for half, side in enumerate((left, right)):
            lo = max(start, NZ * half)
            hi = min(start + 32, NZ * half + NZ)
            if lo < hi:
                here = (lane >= at + lo - start) & (lane < at + hi - start)
                block = jnp.where(here, turn(side[8 + row : 16 + row, :], at - start), block)
        return block

    for chip in range(4):
        for ty in range(16):
            main = rest = jnp.zeros((8, NZ), F32)
            for g in range(4):
                main = put(main, 32 * chip - 6 + 8 * g, 16 * ty - 8, 32 * g)
                rest = put(rest, 32 * chip + 26 + 3 * g, 16 * ty - 8, 32 * g)
            row = 11 * (16 * chip + ty)
            out_ref[row : row + 8, :] = main
            out_ref[row + 8 : row + 11, :] = rest[0:3]


def split_windows(source, mine, other, arrived, sem):
    core = parity()[0] == 1
    lane = lanes((8, NZ))
    sub = lax.broadcasted_iota(jnp.int32, (8, NZ), 0)
    count = mine.shape[0] // 8
    copy = pltpu.make_async_copy(source.at[pl.ds(0, 11 * count)], arrived.at[pl.ds(0, 11 * count)], sem.at[0])
    copy.start()
    arrived[11 * count : 11 * count + 16, :] = jnp.zeros((16, NZ), F32)
    copy.wait()
    for k in range(count):
        row = 11 * k

        def rows(first):
            return arrived[row + first : row + first + 8, :]

        main = rows(0)
        third = jnp.where(sub < 3, turn(rows(8), 64), jnp.where(sub < 6, turn(rows(5), 32), rows(2)))
        fourth = jnp.where(sub < 1, turn(rows(10), 32), jnp.where(sub < 4, rows(7), 0.0))
        upper = jnp.where(lane < 64, turn(main, 64), jnp.where(lane < 96, third, fourth))
        mine[8 * k : 8 * k + 8, :] = jnp.where(core, upper, main)
        other[8 * k : 8 * k + 8, :] = jnp.where(core, main, upper)


def parity():
    return lax.rem(lax.axis_index("tx"), 2), lax.rem(lax.axis_index("ty"), 2)


def strips(ref, e_ref, o_ref, row, k):
    odd = parity()[1] == 1
    low = ref[:, 0:4, :]
    high = ref[:, 12:16, :]
    e_ref[row : row + T, k : k + 4, :] = jnp.where(odd, low, high)
    o_ref[row : row + T, k : k + 4, :] = jnp.where(odd, high, low)


def shallow_strips(ref, e_ref, o_ref, row, shallow, at):
    odd = parity()[1] == 1
    lane = lanes((T, NZ))
    packed = ref[0]
    for x in range(1, T):
        packed = jnp.where(lane >= SH * x, turn(ref[x], SH * x), packed)
    shallow[at : at + T, :] = packed
    e_ref[row] = jnp.where(odd, packed[0:8], packed[8:16])
    o_ref[row] = jnp.where(odd, packed[8:16], packed[0:8])


def pack_fields(*refs):
    sources, (e_ref, o_ref, shallow), targets, sems = refs[:8], refs[8:11], refs[11:19], refs[19]
    copies = [pltpu.make_async_copy(a, b, sems.at[i]) for i, (a, b) in enumerate(zip(sources, targets))]
    for copy in copies:
        copy.start()
    for f, ref in enumerate(targets[:7]):
        copies[f].wait()
        strips(ref, e_ref, o_ref, T * (f // 2), 4 * (f % 2))
        if f in SHALLOW:
            i = SHALLOW.index(f)
            shallow_strips(ref, e_ref, o_ref, 4 * T + i, shallow, T * i)
    blank = jnp.zeros((T, 4, NZ), F32)
    e_ref[3 * T : 4 * T, 4:8, :] = blank
    o_ref[3 * T : 4 * T, 4:8, :] = blank
    copies[7].wait()


def beside_y(got, f, rows):
    odd = parity()[1] == 1
    slot, k = f // 2, 4 * (f % 2)
    a, b = (strip[rows(T * slot), k : k + 4, :] for strip in got)
    return jnp.where(odd, a, b), jnp.where(odd, b, a)


def shallow_beside_y(got, i):
    odd = parity()[1] == 1
    a, b = (strip[4 * T + i] for strip in got)
    return jnp.where(odd, a, b), jnp.where(odd, b, a)


def pack_x(*refs):
    fields, shallow, got, (e_ref, o_ref) = refs[:7], refs[7], refs[8:10], refs[10:]
    odd_x = parity()[0]
    for f, ref in enumerate(fields):
        width = WIDTHS[f]
        for low, out in ((odd_x, e_ref), (1 - odd_x, o_ref)):
            for q in range(width):
                x = low * q + (1 - low) * (T - 1 - q)
                row, more = OFFSETS[f][q], width - 1 - q
                if more:
                    below, above = beside_y(got, f, lambda start: start + x)
                    out[row : row + more, :] = below[4 - more : 4]
                    out[row + more + T : row + more + T + more, :] = above[0:more]
                out[row + more : row + more + T, :] = ref[x]
    for i in range(len(SHALLOW)):
        row = SHALLOW_ROW + E * i
        below, above = shallow_beside_y(got, i)
        for out in (e_ref, o_ref):
            out[row : row + 8, :] = below
            out[row + 8 : row + 24, :] = shallow[T * i : T * i + T, :]
            out[row + 24 : row + 32, :] = above


def count_planes(wavelet, sx, sy, bits, rx, ry, src_ref, rec_ref, scale_ref):
    x0 = lax.axis_index("tx") * T - T
    y0 = lax.axis_index("ty") * T - H
    for t in range(STEPS):
        scale_ref[t : t + 1, :] = jnp.full((1, NZ), wavelet[t], F32)

    def rows(values):
        grid = lax.broadcasted_iota(jnp.int32, (E, values.shape[1]), 0) + y0
        return jnp.where(grid == values, 1.0, 0.0).astype(F32)

    dims = (((1,), (1,)), ((), ()))
    sign = (2 * bits[...] - 1).astype(F32)
    for values, ys, depth, weight, out in (
        (sx[...], sy[...], SRC_DEPTH, sign, src_ref),
        (rx[...], ry[...], REC_DEPTH, None, rec_ref),
    ):
        left = rows(ys)
        if weight is not None:
            left = left * weight
        grid = lax.broadcasted_iota(jnp.int32, (NZ, values.shape[1]), 0)
        here = grid % SH == depth
        for piece in range(3):
            hit = here & (grid // SH + (x0 + T * piece) == values)
            right = jnp.where(hit, 1.0, 0.0).astype(F32)
            out[piece] = lax.dot_general(left, right, dims, preferred_element_type=F32)


def laplace(ref, x, n, ys, ny):
    rows = pl.ds(x, n)
    lane = lanes((1, 1, NZ))
    center = ref[rows, pl.ds(ys, ny), :]
    total = ref[pl.ds(x + 1, n), pl.ds(ys, ny), :] + ref[pl.ds(x - 1, n), pl.ds(ys, ny), :]
    total = total + ref[rows, pl.ds(ys + 1, ny), :] + ref[rows, pl.ds(ys - 1, ny), :]
    down = jnp.where(lane == NZ - 1, 0.0, turn(center, -1))
    up = jnp.where(lane == 0, 0.0, turn(center, 1))
    return center, total + down + up - 6.0 * center


def shallow_laplace(ref):
    rows = pl.ds(PAD, E)
    lane = lanes((1, 1, NZ))
    depth = lane & (SH - 1)
    center = ref[:, rows, :]
    total = ref[:, pl.ds(PAD + 1, E), :] + ref[:, pl.ds(PAD - 1, E), :]
    total = total + jnp.where(depth == SH - 1, 0.0, turn(center, -1))
    total = total + jnp.where(depth == 0, 0.0, turn(center, 1))
    left = turn(center, SH)
    right = turn(center, -SH)
    none = jnp.zeros((1, E, NZ), F32)
    left = jnp.where(lane < SH, jnp.concatenate([none, left[0:2]], 0), left)
    right = jnp.where(lane >= NZ - SH, jnp.concatenate([right[1:3], none], 0), right)
    return center, total + left + right - 6.0 * center


def loop(start, blocks, n, body):
    for i in range(blocks):
        body(XO + start + i * n)


ALL_Y = pl.ds(PAD, G)
OWN_Y = pl.ds(PAD + D, T)
OWN_X = pl.ds(XO + D, T)
PLAN = ((0, 4, 6), (2, 5, 4), (3, 3, 6), (4, 4, 4))
WIDE = (G + 2 * XO, G + 2 * PAD, NZ)
FLAT = (G + 2 * XO, G, NZ)
LOW = (3, E + 2 * PAD, NZ)


def clear_ends(ref):
    blank = jnp.zeros((3, PAD, NZ), F32)
    ref[:, 0:PAD, :] = blank
    ref[:, PAD + E : PAD + E + PAD, :] = blank


def assemble(f, ref, ext, got, xe, xo):
    odd = parity()[0] == 1
    ext[OWN_X, OWN_Y, :] = ref[...]
    below, above = beside_y(got, f, lambda start: slice(start, start + T))
    ext[OWN_X, PAD : PAD + 4, :] = below
    ext[OWN_X, PAD + 20 : PAD + 24, :] = above
    for q, length in enumerate(LENGTHS[f]):
        rows = pl.ds(OFFSETS[f][q], length)
        at = pl.ds(PAD + D - (length - T) // 2, length)
        got_e = xe[rows, :]
        got_o = xo[rows, :]
        ext[XO + D - 1 - q, at, :] = jnp.where(odd, got_e, got_o)
        ext[XO + D + T + q, at, :] = jnp.where(odd, got_o, got_e)


def assemble_shallow(i, mine, ext, got, xe, xo):
    odd = parity()[0] == 1
    rows = pl.ds(SHALLOW_ROW + E * i, E)
    got_e = xe[rows, :]
    got_o = xo[rows, :]
    ext[0, PAD : PAD + E, :] = jnp.where(odd, got_e, got_o)
    ext[2, PAD : PAD + E, :] = jnp.where(odd, got_o, got_e)
    ext[1, PAD + H : PAD + H + T, :] = mine
    below, above = shallow_beside_y(got, i)
    ext[1, PAD : PAD + H, :] = below
    ext[1, PAD + H + T : PAD + E, :] = above


def background(x, n, scale, now, old, C, SF, t):
    rows = pl.ds(x, n)
    center, lap = laplace(now, x, n, PAD, G)
    accel = C[rows, ALL_Y, :] * lap + scale * SF[rows]
    if t < STEPS - 1:
        old[rows, ALL_Y, :] = 2.0 * center - old[rows, ALL_Y, :] + accel
    return accel


def place_sources(src, SF):
    short = lanes((G, NZ))
    for x in range(1, G - 1):
        piece, at = (x - D + T) // T, SH * ((x - D) % T)
        SF[XO + x] = jnp.where(short == SRC_DEPTH, turn(src[piece, 4:28, :], -at), 0.0)


def free(scales, *refs):
    fields, shallow, got, refs = refs[:7], refs[7], refs[8:10], refs[10:]
    xe, xo, src, SA, CS, BS0, BS1, first, second, image = refs[:10]
    U0, U1, C, M0, M1, Q0, Q1, SF, A, US, IM = refs[10:]
    rows = pl.ds(PAD, E)

    with jax.named_scope("assemble"):
        for f, ext in ((0, U0), (2, C), (3, M0), (4, U1), (6, M1)):
            assemble(f, fields[f], ext, got, xe, xo)
        for ext in (US.at[0], US.at[1], BS0, BS1):
            clear_ends(ext)
        for i, ext in enumerate((US.at[0], BS1, CS, US.at[1], BS0)):
            assemble_shallow(i, shallow[T * i : T * i + T, :], ext, got, xe, xo)
        place_sources(src, SF)

    with jax.named_scope("shallow"):
        for t in range(STEPS):
            now, old = US.at[t % 2], US.at[1 - t % 2]
            center, lap = shallow_laplace(now)
            accel = CS[:, rows, :] * lap + scales[t : t + 1, :][None] * src[...]
            SA[t] = accel
            if t < STEPS - 1:
                old[:, rows, :] = 2.0 * center - old[:, rows, :] + accel

    waves = (U1, U0)
    for t in range(STEPS):
        with jax.named_scope("forward"):
            old, now = waves
            scale = scales[t : t + 1, :][None]
            start, blocks, n = PLAN[t]

            def forward(x):
                A[t, pl.ds(x, n)] = background(x, n, scale, now, old, C, SF, t)

            loop(start, blocks, n, forward)
            waves = (now, old)

    def scaled(x):
        rows = pl.ds(x, 6)
        Q0[rows, ALL_Y, :] = C[rows, ALL_Y, :] * M0[rows, ALL_Y, :]

    loop(0, 4, 6, scaled)
    upcoming, latest, q_now, q_new = M0, M1, Q0, Q1
    for t in range(STEPS, 1, -1):
        with jax.named_scope("adjoint"):
            start, blocks, n = PLAN[STEPS - t]

            def back(x):
                rows = pl.ds(x, n)
                _, lap = laplace(q_now, x, n, PAD, G)
                current = 2.0 * upcoming[rows, ALL_Y, :] - latest[rows, ALL_Y, :] + lap
                latest[rows, ALL_Y, :] = current
                q_new[rows, ALL_Y, :] = C[rows, ALL_Y, :] * current

            loop(start, blocks, n, back)
            upcoming, latest = latest, upcoming
            q_now, q_new = q_new, q_now

            def gather(x):
                rows = pl.ds(x, 4)
                mine = pl.ds(x - XO - D, 4)
                product = A[t - 1, rows, D : D + T, :] * upcoming[rows, OWN_Y, :]
                IM[mine] = -product if t == STEPS else IM[mine] - product

            loop(D, 4, 4, gather)

    def finish(x):
        rows = pl.ds(x, 4)
        mine = pl.ds(x - XO - D, 4)
        _, lap = laplace(q_now, x, 4, PAD + D, T)
        ahead = upcoming[rows, OWN_Y, :]
        current = 2.0 * ahead - latest[rows, OWN_Y, :] + lap
        first[mine] = current
        second[mine] = ahead
        IM[mine] = IM[mine] - A[0, rows, D : D + T, :] * current

    loop(D, 4, 4, finish)
    for half in range(2):
        image[pl.ds(half, 128, stride=2), :] = IM[8 * half : 8 * half + 8].reshape(128, NZ).T


def meet(SA, CS, BS0, BS1, free_image, mine, got, rec, image, sent, BS, PS, QS, low, sems):
    deep = [
        pltpu.make_async_copy(
            free_image.at[pl.ds(2 * SH, 256 - 2 * SH)],
            image.at[pl.ds(256 * shot + 2 * SH, 256 - 2 * SH)],
            sems.at[shot],
        )
        for shot in range(2)
    ]
    for copy in deep:
        copy.start()
    rows = pl.ds(PAD, E)
    with jax.named_scope("turn"):
        core = parity()[0] == 1
        planes = [jnp.where(core, got[pl.ds(s, SH, stride=8), :], mine[pl.ds(s, SH, stride=8), :]) for s in range(8)]
        planes = jnp.concatenate(planes, 0)
        turned = jnp.concatenate([planes, jnp.zeros((64, NZ), F32)], 0).T
        parts = [turned[32 * g : 32 * g + 32, :] for g in range(4)]
        flat = lanes((E, NZ))
        pairs = [jnp.where(flat < 64, parts[2 * i], turn(parts[2 * i + 1], 64)) for i in range(2)]
        at = SH * (T - 6)
        PS[0] = turn(pairs[0], at)
        PS[1] = jnp.where(flat < at, turn(pairs[0], at), turn(pairs[1], at))
        PS[2] = turn(pairs[1], at)

    with jax.named_scope("shallow"):
        for i in range(STEPS):
            clear_ends(BS.at[i])
        for i in range(2):
            clear_ends(QS.at[i])
        olds = (BS0, BS1, BS.at[0], BS.at[1], BS.at[2], BS.at[3])
        for t in range(STEPS):
            center, lap = shallow_laplace(olds[t + 1])
            olds[t + 2][:, rows, :] = (
                2.0 * center - olds[t][:, rows, :] + CS[:, rows, :] * lap - PS[...] * SA[t]
            )
        own = pl.ds(H, T)
        now = rec[...] * BS[3, :, rows, :]
        older = None
        delta = -SA[3, 1, own, :] * now[1, H : H + T, :]
        for t in (3, 2, 1):
            QS[t % 2, :, rows, :] = CS[:, rows, :] * now
            _, lap = shallow_laplace(QS.at[t % 2])
            new = 2.0 * now + lap + rec[...] * BS[t - 1, :, rows, :]
            if older is not None:
                new = new - older
            now, older = new, now
            delta = delta - SA[t - 1, 1, own, :] * now[1, H : H + T, :]
        sent[0] = now[1, H : H + T, :]
        sent[1] = older[1, H : H + T, :]

    with jax.named_scope("image"):
        turned = jnp.concatenate([delta, jnp.zeros((NZ - T, NZ), F32)], 0).T
        lane = lanes((SH, NZ))
        for half in range(2):
            line = jnp.zeros((SH, NZ), F32)
            for k in range(8):
                x = 8 * half + k
                piece = turn(turned[SH * x : SH * x + SH, :], 16 * k)
                line = jnp.where((lane >= 16 * k) & (lane < 16 * k + 16), piece, line)
            low[pl.ds(half, SH, stride=2), :] = free_image[pl.ds(half, SH, stride=2), :] + line
        shallow = [
            pltpu.make_async_copy(low, image.at[pl.ds(256 * shot, 2 * SH)], sems.at[2 + shot]) for shot in range(2)
        ]
        for copy in shallow:
            copy.start()
        for copy in (*deep, *shallow):
            copy.wait()


def born(scales, *refs):
    fields, got, refs = refs[:7], refs[7:9], refs[9:]
    xe, xo, src, near, far, first0, second0, sent, last, before, first, second, U0, U1, C, PT, B, SF = refs
    for f, ext in ((0, U0), (1, B.at[1]), (2, C), (4, U1), (5, B.at[0])):
        assemble(f, fields[f], ext, got, xe, xo)
    place_sources(src, SF)
    core = parity()[0] == 1
    for s in range(8):
        planes = []
        for k in range(4):
            rows = pl.ds(128 * k + s, T, stride=8)
            a, b = near[rows, :], far[rows, :]
            planes += [jnp.where(core, b, a), jnp.where(core, a, b)]
        turned = jnp.concatenate(planes, 0).T
        for g in range(4):
            PT[8 * g + s] = turned[32 * g : 32 * g + 32, :]
    waves = (U1, U0)
    for t in range(STEPS):
        old, now = waves
        scale = scales[t : t + 1, :][None]
        start, blocks, n = PLAN[t]

        def step(x):
            rows = pl.ds(x, n)
            accel = background(x, n, scale, now, old, C, SF, t)
            center, lap = laplace(B.at[t + 1], x, n, PAD, G)
            B[t + 2, rows, ALL_Y, :] = (
                2.0 * center - B[t, rows, ALL_Y, :] + C[rows, ALL_Y, :] * lap
                - PT[pl.ds(x - XO + 2, n), 4:28, :] * accel
            )

        loop(start, blocks, n, step)
        waves = (now, old)
    last[...] = B[STEPS + 1, OWN_X, OWN_Y, :]
    before[...] = B[STEPS, OWN_X, OWN_Y, :]
    here = lanes((T, NZ)) < SH
    for x in range(T):
        first[x] = first0[x] + jnp.where(here, turn(sent[0], -SH * x), 0.0)
        second[x] = second0[x] + jnp.where(here, turn(sent[1], -SH * x), 0.0)


def arrange(arrived, out):
    first = lax.axis_index("shot") * 16
    lane = lanes((8, NZ))
    for half in range(2):
        groups = []
        for j in range(8):
            groups.append(
                arrived[pl.ds(first + 2 * j + half, 8, stride=32), :]
                + arrived[pl.ds(first + 256 + 2 * j + half, 8, stride=32), :]
            )
        for k in range(8):
            line = jnp.zeros((8, NZ), F32)
            for j in range(8):
                line = jnp.where((lane >= 16 * j) & (lane < 16 * j + 16), turn(groups[j], 16 * j - 16 * k), line)
            out[pl.ds(8 * half + k, 8, stride=16), :] = line


def swap(cells, axis, odd):
    count = lax.axis_size(axis)
    pairs = [(i, ((i - odd) ^ 1) + odd) for i in range(odd, count - odd)]
    return lax.ppermute(cells, axis, pairs)


def per_device(
    perturbation, courant_sq, background_prev, background_now, born_prev, born_now,
    adjoint_next, adjoint_after, encode_bits, wavelet, source_x, source_y, receiver_x, receiver_y,
):
    shape = lambda *dims: jax.ShapeDtypeStruct(dims, F32)
    tile = (T, T, NZ)
    fields = [
        a.reshape(tile)
        for a in (background_now, born_now, courant_sq, adjoint_next, background_prev, born_prev, adjoint_after)
    ]

    strip = shape(*STRIP_Y)
    send_e, send_o, shallow, *fields, plane = call(
        pack_fields,
        (strip, strip, shape(5 * T, NZ)) + (shape(*tile),) * 7 + (shape(128, 256),),
        [HBM] * 8,
        [pltpu.SemaphoreType.DMA((8,))],
    )(*[pltpu.with_memory_space_constraint(a, pltpu.HBM) for a in (*fields, perturbation.reshape(128, 256))])
    got_o = swap(send_o, "ty", 1)
    got = (swap(send_e, "ty", 0), got_o)
    side = pltpu.VMEM((160, NZ), F32)
    blocks = call(pack_windows, shape(704, NZ), [VMEM], [side, side])(plane)
    groups = [[(2 * chip + core) * 16 + ty for chip in range(4) for ty in range(16)] for core in range(2)]
    windows = lax.all_to_all(
        blocks.reshape(704, 1, NZ), ("tx", "ty"), split_axis=0, concat_axis=0, tiled=True, axis_index_groups=groups
    ).reshape(704, NZ)
    pieces = shape(3, E, NZ)
    src, rec, scales = call(count_planes, (pieces, pieces, shape(8, NZ)), [SMEM] + [VMEM] * 5)(
        wavelet, source_x[None], source_y[None], encode_bits, receiver_x[None], receiver_y[None]
    )
    strip = shape(*STRIP_X)
    send_e, send_o = call(pack_x, (strip, strip), [VMEM] * 10, cost=BUSY)(*fields, shallow, *got)
    across_o = swap(send_o, "tx", 1)
    across = (swap(send_e, "tx", 0), across_o)
    one = lambda *dims: pltpu.VMEM(dims, F32)
    cells = shape(*tile)
    low = shape(*LOW)
    SA, CS, BS0, BS1, first, second, image = call(
        free,
        (shape(STEPS, 3, E, NZ), low, low, low, cells, cells, shape(256, NZ)),
        [VMEM] * 14,
        [one(*WIDE)] * 7 + [one(*FLAT), one(STEPS, *FLAT), one(2, *LOW), one(*tile)],
    )(scales, *fields, shallow, *got, *across, src)
    sems = lambda n: pltpu.SemaphoreType.DMA((n,))

    def split(windows, count):
        return call(split_windows, (shape(8 * count, NZ),) * 2, [HBM], [one(11 * count + 16, NZ), sems(1)])(
            pltpu.with_memory_space_constraint(windows, pltpu.HBM)
        )

    windows, src = lax.optimization_barrier((windows, src))
    near, other = split(windows, SH)
    far = swap(other, "tx", 0)
    image, sent = call(
        meet,
        (shape(512, NZ), shape(2, T, NZ)),
        [VMEM] * 8,
        [one(4, *LOW), one(3, E, NZ), one(2, *LOW), one(2 * SH, NZ), sems(4)],
        places=(HBM, VMEM),
    )(SA, CS, BS0, BS1, image, near, far, rec)
    windows, image = lax.optimization_barrier((windows, image))
    near, other = split(windows, 64)
    far = swap(other, "tx", 0)
    last, before, first, second = call(
        born,
        (cells, cells, cells, cells),
        [VMEM] * 18,
        [one(*WIDE)] * 3 + [one(E, E, NZ), one(STEPS + 2, *WIDE), one(*FLAT)],
    )(scales, *fields, *got, *across, src, near, far, first, second, sent)

    arrived = lax.all_to_all(
        image.reshape(256, 2, NZ), ("shot", "tx", "ty"), split_axis=0, concat_axis=0, tiled=True
    )
    hessian = call(arrange, shape(128, NZ), [VMEM])(arrived.reshape(512, NZ))
    return (hessian[None], first[None], second[None], last[None], before[None])


def solution(mesh):
    field = P("shot", "tx", "ty", None)
    placed = (
        P(("tx", "ty"), None, None),
        P("tx", "ty", None),
        field, field, field, field, field, field,
        P("shot", None),
        P(), P(), P(), P(), P(),
    )
    return jax.shard_map(
        per_device,
        mesh=mesh,
        in_specs=placed,
        out_specs=(P(("tx", "ty"), None, "shot"), field, field, field, field),
        check_vma=False,
    )
```
